256 devices in a mesh: ctx: 128 (over x, z, y), head: 2 (over core).
Axes of the slice: x: 4, y: 4, z: 8, core: 2. Of those that a mesh axis runs over, the one named last changes fastest.
Arguments:
- queries: bfloat16 [16384, 256], P('ctx', 'head'), may hold values from -100 to 100
- keys: bfloat16 [16384, 256], P('ctx', 'head'), may hold values from -5 to 5
- values: bfloat16 [16384, 256], P('ctx', 'head'), may hold values from -6 to 6
- picks: int32 [2, 128, 2], P('head'), may hold values from 0 to 6, as said below
- out_weight: bfloat16 [256, 4096], P('head'), may hold values from -0.375 to 0.375
Outputs:
- mixed: bfloat16 [16384, 4096], P('ctx', 'head')
The draws below stay inside these ranges and needn't reach their ends.
Inputs may be any that keep to these rules, and one draw needn't show every extreme that they name: `picks`: an entry not below its block's own span (b * 128 // 2048 for block b) is ignored; where the own span is 2 or more, both entries of a block are below it and differ.
All inputs are finite; a program needn't handle non-finite values.
Results may differ from the reference program's by a relative error of at most 0.012.
Values may be sent and summed in bfloat16 or wider, within the bound.
A program may use at most 64 MiB of HBM per device.

```python
import jax
import jax.numpy as jnp
from jax import lax

HD = 128
HEADS = 2
D = 4096
SPAN = 2048
QBLK = 128
TOKENS = 16384
NBLK = 128


def shared_keys(key):
    return jnp.clip(jax.random.normal(key, (TOKENS, HEADS * HD), jnp.float32), -5.0, 5.0)


def draw_keys(key, part):
    base = shared_keys(key)
    return base.astype(jnp.bfloat16)


def draw_queries(key, part):
    key = jax.random.fold_in(key, 7)
    first = jax.random.fold_in(key, 0)
    return jnp.clip(jax.random.normal(first, (TOKENS, HEADS * HD), jnp.float32), -5.0, 5.0).astype(jnp.bfloat16)


def draw_picks(key, part):
    key = jax.random.fold_in(key, 3)
    streams = jax.random.split(key, 5)
    block = jnp.arange(NBLK, dtype=jnp.int32)
    own_span = block * QBLK // SPAN
    shape = (HEADS, NBLK)
    upper = jnp.broadcast_to(jnp.maximum(own_span, 1), shape)
    draws = [jax.random.randint(streams[number], shape, 0, upper) for number in range(4)]
    first = jnp.minimum(draws[0], draws[1])
    second = jnp.minimum(draws[2], draws[3])
    offset = jax.random.randint(streams[4], shape, 0, jnp.broadcast_to(jnp.maximum(own_span - 1, 1), shape))
    second = jnp.where(second == first, (first + 1 + offset) % upper, second)
    final = block == NBLK - 1
    second = jnp.where(final, own_span - 1, second)
    first = jnp.where(final & (first == own_span - 1), jnp.maximum(own_span - 2, 0), first)
    second = jnp.where(own_span <= 1, own_span, second)
    return jnp.stack([first, second], axis=-1).astype(jnp.int32)


def steps_of(stream_key, dims, shards, smallest, top_value):
    def one(dim, shards_of):
        steps = jax.random.uniform(jax.random.fold_in(jax.random.fold_in(stream_key, 6), dim), (shards_of,), jnp.float32, smallest / len(shards), top_value / len(shards))
        return jnp.repeat(jnp.exp(steps), dims[dim] // shards_of).reshape((-1,) + (1,) * (len(dims) - dim - 1))

    factor_of = one(*shards[0])
    for cut in shards[1:]:
        factor_of = factor_of * one(*cut)
    return factor_of


def normal_values(stream_key, extent, deviation, most, cuts=(), kind=jnp.bfloat16):
    entries = deviation * jax.random.normal(stream_key, extent, jnp.float32)
    if cuts:
        entries = entries * steps_of(stream_key, extent, cuts, -0.22, 0.18)
    return jnp.clip(entries, -most, most).astype(kind)


def setup_inputs(seed: int = 0) -> dict:
    key_list = jax.random.split(jax.random.key(seed), 6)
    queries = draw_queries(jax.random.fold_in(key_list[5], 71), 0)
    keys = draw_keys(jax.random.fold_in(key_list[5], 71), 0)
    values = normal_values(key_list[2], (TOKENS, HEADS * HD), 1.0, 6.0, ((0, 128), (1, 2)))
    picks = draw_picks(jax.random.fold_in(key_list[5], 71), 0)
    out_weight = normal_values(key_list[4], (HEADS * HD, D), (HEADS * HD) ** -0.5, 0.375, ((0, 2),))
    return dict(queries=queries, keys=keys, values=values, picks=picks, out_weight=out_weight)


def attend_block(block, queries, key_heads, value_heads, picks):
    own_span = block * QBLK // SPAN
    query_rows = lax.dynamic_slice_in_dim(queries, block * QBLK, QBLK, 0)
    query_pos = block * QBLK + jnp.arange(QBLK, dtype=jnp.int32)
    results = []
    for head in range(HEADS):
        query_head = query_rows[:, head * HD:(head + 1) * HD].astype(jnp.float32)
        anchors = [own_span, picks[head, block, 0], picks[head, block, 1]]
        key_parts = []
        value_parts = []
        valid_parts = []
        for which, anchor in enumerate(anchors):
            first_row = (anchor * SPAN).astype(jnp.int32)
            key_parts.append(lax.dynamic_slice_in_dim(key_heads[head], first_row, SPAN, 0))
            value_parts.append(lax.dynamic_slice_in_dim(value_heads[head], first_row, SPAN, 0))
            key_pos = first_row + jnp.arange(SPAN, dtype=jnp.int32)
            if which == 0:
                valid_parts.append(key_pos[None, :] <= query_pos[:, None])
            else:
                valid_parts.append(jnp.broadcast_to(anchor < own_span, (QBLK, SPAN)))
        key_cat = jnp.concatenate(key_parts, axis=0).astype(jnp.float32)
        value_cat = jnp.concatenate(value_parts, axis=0)
        valid = jnp.concatenate(valid_parts, axis=1)
        scores = jnp.einsum('td,sd->ts', query_head, key_cat) / jnp.sqrt(jnp.float32(HD))
        top = lax.optimization_barrier(jnp.max(jnp.where(valid, scores, -jnp.inf), axis=1, keepdims=True))
        weights = jnp.where(valid, jnp.exp(scores - top), jnp.float32(0.0))
        total = lax.optimization_barrier(jnp.sum(weights, axis=1, keepdims=True))
        numer = jnp.dot(weights.astype(jnp.bfloat16), value_cat, preferred_element_type=jnp.float32)
        results.append(numer / total)
    return jnp.concatenate(results, axis=1).astype(jnp.bfloat16)

def reference(queries, keys, values, picks, out_weight):
    key_heads = keys.reshape(TOKENS, HEADS, HD).transpose(1, 0, 2)
    value_heads = values.reshape(TOKENS, HEADS, HD).transpose(1, 0, 2)
    blocks = jnp.arange(NBLK, dtype=jnp.int32)
    attended = lax.map(lambda block: attend_block(block, queries, key_heads, value_heads, picks), blocks)
    attended = attended.reshape(TOKENS, HEADS * HD)
    return jnp.dot(attended, out_weight, preferred_element_type=jnp.float32).astype(jnp.bfloat16)
```

```python
import functools
import math

import jax
import jax.numpy as jnp
from jax import lax
from jax.experimental import pallas as pl
from jax.experimental.pallas import tpu as pltpu
from jax.sharding import PartitionSpec as P

BLK = 128
SPANS = 8
ZN = 4
YN = 4
GROUP = ZN * YN
CHUNK = YN * BLK
COLS = 2048
NEGATIVE = -1e30
RATE = math.log2(math.e) / math.sqrt(128.0)
MESH = pl.DeviceIdType.MESH


def kernel(
    q_hbm, k_hbm, v_hbm, picks_hbm, w_hbm, out_ref,
    picks, kbuf, vbuf, qbuf, vraw, pout, sout, pin, sin, wbuf, att, top, total, acc,
    local_sem, z_send, z_recv, y_send, y_recv, q_send, q_recv, p_send, p_recv, h_send, h_recv,
):
    ctx = lax.axis_index("ctx")
    head = lax.axis_index("head")
    span = ctx // GROUP
    z = (ctx % GROUP) // YN
    y = ctx % YN
    right, left = (y + 1) % YN, (y + YN - 1) % YN
    z_peer = [z, z + 1 - 2 * (z % 2), (z + 2) % ZN, ZN - 1 - z]
    other = 1 - head

    def device(to_span, to_z, to_y):
        return (to_span * GROUP + to_z * YN + to_y, head)

    def remote(src, dst, send, recv, to):
        return pltpu.make_async_remote_copy(
            src_ref=src, dst_ref=dst, send_sem=send, recv_sem=recv, device_id=to, device_id_type=MESH
        )

    mine = [
        pltpu.make_async_copy(v_hbm, vraw, local_sem.at[0]),
        pltpu.make_async_copy(k_hbm, kbuf.at[0, y], local_sem.at[1]),
        pltpu.make_async_copy(q_hbm, qbuf.at[0], local_sem.at[2]),
        pltpu.make_async_copy(
            w_hbm.at[:, pl.ds(pl.multiple_of(head * COLS, COLS), COLS)], wbuf.at[0], local_sem.at[3]
        ),
        pltpu.make_async_copy(picks_hbm, picks, local_sem.at[4]),
    ]
    for copy in mine:
        copy.start()

    barrier = pltpu.get_barrier_semaphore()
    greeted = [device(span, z_peer[i], y) for i in range(1, ZN)]
    greeted += [device(span, z, right), device(span, z, left)]
    greeted += [device((span + d) % SPANS, z, y) for d in range(1, SPANS)]
    greeted += [(ctx, other)]
    for peer in greeted:
        pl.semaphore_signal(barrier, inc=1, device_id=peer, device_id_type=MESH)

    for v in range(1, SPANS):
        @pl.when(span + v >= SPANS)
        def _():
            qbuf[v] = jnp.zeros((BLK, BLK), jnp.bfloat16)

    mine[0].wait()
    vbuf[0, y] = vraw[...].T
    mine[1].wait()
    mine[2].wait()
    pl.semaphore_wait(barrier, len(greeted))

    def z_copy(i, which):
        buf = (kbuf, vbuf)[which]
        return remote(
            buf.at[0, y], buf.at[i, y], z_send.at[i, which], z_recv.at[i, which], device(span, z_peer[i], y)
        )

    def y_copies(i):
        at_right, at_left = device(span, z, right), device(span, z, left)
        return [
            remote(kbuf.at[i, y], kbuf.at[i, y], y_send.at[i, 0], y_recv.at[i, 0], at_right),
            remote(vbuf.at[i, y], vbuf.at[i, y], y_send.at[i, 3], y_recv.at[i, 3], at_left),
            remote(kbuf.at[i, y], kbuf.at[i, y], y_send.at[i, 1], y_recv.at[i, 1], at_left),
            remote(vbuf.at[i, y], vbuf.at[i, y], y_send.at[i, 2], y_recv.at[i, 2], at_right),
        ]

    def relays(i):
        return [
            remote(
                kbuf.at[i, left], kbuf.at[i, left], y_send.at[i, 4], y_recv.at[i, 4], device(span, z, right)
            ),
            remote(
                vbuf.at[i, right], vbuf.at[i, right], y_send.at[i, 5], y_recv.at[i, 5], device(span, z, left)
            ),
        ]

    def q_copy(v):
        return remote(
            qbuf.at[0], qbuf.at[v], q_send.at[v], q_recv.at[v], device((span + SPANS - v) % SPANS, z, y)
        )

    def p_copies(v):
        home = device((span + v) % SPANS, z, y)
        return [
            remote(pout.at[v], pin.at[v], p_send.at[v, 0], p_recv.at[v, 0], home),
            remote(sout.at[v], sin.at[v], p_send.at[v, 1], p_recv.at[v, 1], home),
        ]

    w_copy = remote(
        w_hbm.at[:, pl.ds(pl.multiple_of(other * COLS, COLS), COLS)],
        wbuf.at[1], h_send.at[0], h_recv.at[0], (ctx, other),
    )
    att_copy = remote(att.at[0], att.at[1], h_send.at[1], h_recv.at[1], (ctx, other))

    def spread(i):
        if i:
            z_copy(i, 0).wait_recv()
            z_copy(i, 1).wait_recv()
        for copy in y_copies(i):
            copy.start()

    def pass_on(i):
        from_near = y_copies(i)
        onward = relays(i)
        from_near[0].wait_recv()
        onward[0].start()
        from_near[1].wait_recv()
        onward[1].start()

    def arrive(i):
        from_near = y_copies(i)
        from_near[2].wait_recv()
        from_near[3].wait_recv()
        for copy in relays(i):
            copy.wait_recv()

    def attend(i, p, masked):
        queries = qbuf[pl.ds(2 * p, 2)].reshape(2 * BLK, BLK)
        keys = kbuf[i].reshape(CHUNK, BLK)
        scores = lax.dot_general(
            keys, queries, (((1,), (1,)), ((), ())), preferred_element_type=jnp.float32
        )
        if masked:
            key = lax.broadcasted_iota(jnp.int32, (CHUNK, 2 * BLK), 0)
            token = lax.broadcasted_iota(jnp.int32, (CHUNK, 2 * BLK), 1)
            if i == 0:
                last = y * BLK + token
            else:
                last = jnp.where(z_peer[i] < z, CHUNK, -1)
            allowed = (token >= BLK) | (key <= last)
            scores = jnp.where(allowed, scores, NEGATIVE)
        high = jnp.max(scores, axis=0, keepdims=True)
        if i:
            high = jnp.maximum(high, top[p])
        weights = jnp.exp2((scores - high) * RATE)
        part = jnp.sum(weights, axis=0, keepdims=True)
        values = jnp.concatenate([vbuf[i, b] for b in range(YN)], axis=1)
        numer = jnp.dot(values, weights.astype(jnp.bfloat16), preferred_element_type=jnp.float32)
        if i:
            fade = jnp.exp2((top[p] - high) * RATE)
            part = part + total[p] * fade
            numer = numer + acc[p] * fade
        top[p] = high
        total[p] = part
        acc[p] = numer

    def finish(p):
        for side in range(2):
            v = 2 * p + side
            lanes = slice(side * BLK, (side + 1) * BLK)

            @pl.when((v >= 1) & (span + v < SPANS))
            def _():
                part = total[p, :, lanes]
                pout[v] = (acc[p, :, lanes] / part).astype(jnp.bfloat16)
                sout[v, 0:4] = jnp.broadcast_to(top[p, :, lanes], (4, BLK))
                sout[v, 4:8] = jnp.broadcast_to(part, (4, BLK))
                for copy in p_copies(v):
                    copy.start()

    pairs = (SPANS - span + 1) // 2

    def compute(i):
        arrive(i)
        attend(i, 0, True)
        if i == ZN - 1:
            finish(0)

        def body(p, carry):
            attend(i, p, False)
            if i == ZN - 1:
                finish(p)
            return carry

        lax.fori_loop(1, pairs, body, 0)

    z_copy(1, 0).start()
    z_copy(1, 1).start()
    spread(0)
    for i in range(2, ZN):
        z_copy(i, 0).start()
        z_copy(i, 1).start()
    for v in range(1, SPANS):
        @pl.when(span >= v)
        def _():
            q_copy(v).start()
    w_copy.start()
    pass_on(0)
    spread(1)
    for v in range(1, SPANS):
        @pl.when(span + v < SPANS)
        def _():
            q_copy(v).wait_recv()
    compute(0)
    for i in range(1, ZN):
        pass_on(i)
        if i + 1 < ZN:
            spread(i + 1)
        compute(i)

    mine[4].wait()
    def gather(u, carry):
        for copy in p_copies(u):
            copy.wait_recv()
        which = span - u
        picked = (picks[0, 0, ctx] == which) | (picks[0, 1, ctx] == which)
        theirs = jnp.where(picked, sin[u, 0:1], NEGATIVE)
        ours = top[0, :, 0:BLK]
        high = jnp.maximum(ours, theirs)
        fade = jnp.exp2((ours - high) * RATE)
        share = sin[u, 4:5] * jnp.exp2((theirs - high) * RATE)
        top[0, :, 0:BLK] = high
        total[0, :, 0:BLK] = total[0, :, 0:BLK] * fade + share
        acc[0, :, 0:BLK] = acc[0, :, 0:BLK] * fade + pin[u].astype(jnp.float32) * share
        return carry

    lax.fori_loop(1, span + 1, gather, 0)
    att[0] = (acc[0, :, 0:BLK] / total[0, :, 0:BLK]).T.astype(jnp.bfloat16)
    att_copy.start()
    mine[3].wait()
    w_copy.wait_recv()
    att_copy.wait_recv()
    attended = jnp.concatenate([att[0], att[1]], axis=1)
    wide = 512

    def project(n, carry):
        columns = pl.ds(pl.multiple_of(n * wide, wide), wide)
        weight = wbuf[:, :, columns].reshape(2 * BLK, wide)
        out_ref[:, columns] = jnp.dot(attended, weight, preferred_element_type=jnp.float32).astype(jnp.bfloat16)
        return carry

    lax.fori_loop(0, COLS // wide, project, 0)

    for i in range(ZN):
        if i:
            z_copy(i, 0).wait_send()
            z_copy(i, 1).wait_send()
        for copy in y_copies(i) + relays(i):
            copy.wait_send()
    for v in range(1, SPANS):
        @pl.when(span >= v)
        def _():
            q_copy(v).wait_send()

        @pl.when(span + v < SPANS)
        def _():
            for copy in p_copies(v):
                copy.wait_send()
    w_copy.wait_send()
    att_copy.wait_send()


def local(queries, keys, values, picks, out_weight):
    hbm = pl.BlockSpec(memory_space=pltpu.HBM)
    dma = pltpu.SemaphoreType.DMA
    bf16, f32 = jnp.bfloat16, jnp.float32
    return pl.pallas_call(
        kernel,
        out_shape=jax.ShapeDtypeStruct((BLK, COLS), bf16),
        in_specs=[hbm] * 5,
        out_specs=pl.BlockSpec(memory_space=pltpu.VMEM),
        scratch_shapes=[
            pltpu.SMEM((1, 2, BLK), jnp.int32),
            pltpu.VMEM((ZN, YN, BLK, BLK), bf16),
            pltpu.VMEM((ZN, YN, BLK, BLK), bf16),
            pltpu.VMEM((SPANS, BLK, BLK), bf16),
            pltpu.VMEM((BLK, BLK), bf16),
            pltpu.VMEM((SPANS, BLK, BLK), bf16),
            pltpu.VMEM((SPANS, 8, BLK), f32),
            pltpu.VMEM((SPANS, BLK, BLK), bf16),
            pltpu.VMEM((SPANS, 8, BLK), f32),
            pltpu.VMEM((2, BLK, COLS), bf16),
            pltpu.VMEM((2, BLK, BLK), bf16),
            pltpu.VMEM((SPANS // 2, 1, 2 * BLK), f32),
            pltpu.VMEM((SPANS // 2, 1, 2 * BLK), f32),
            pltpu.VMEM((SPANS // 2, BLK, 2 * BLK), f32),
            dma((5,)),
            dma((ZN, 2)),
            dma((ZN, 2)),
            dma((ZN, 6)),
            dma((ZN, 6)),
            dma((SPANS,)),
            dma((SPANS,)),
            dma((SPANS, 2)),
            dma((SPANS, 2)),
            dma((2,)),
            dma((2,)),
        ],
        compiler_params=pltpu.CompilerParams(
            collective_id=0, has_side_effects=True, vmem_limit_bytes=56 * 1024 * 1024
        ),
        cost_estimate=pl.CostEstimate(flops=2**30, bytes_accessed=2**22, transcendentals=2**21),
    )(queries, keys, values, jnp.swapaxes(picks, 1, 2), out_weight)


def solution(mesh):
    placed = (
        P("ctx", "head"),
        P("ctx", "head"),
        P("ctx", "head"),
        P("head", None, None),
        P("head", None),
    )
    return jax.shard_map(
        local, mesh=mesh, in_specs=placed, out_specs=P("ctx", "head"), check_vma=False
    )
```

```python
import math

import jax
import jax.numpy as jnp
from jax import lax
from jax.experimental import pallas as pl
from jax.experimental.pallas import tpu as pltpu
from jax.sharding import PartitionSpec as P

BLK = 128
XN = 4
YN = 4
MATES = 4
SLOTS = XN * MATES
CHUNK = YN * BLK
COLS = 2048
NEGATIVE = -1e30
RATE = math.log2(math.e) / math.sqrt(128.0)
MESH = pl.DeviceIdType.MESH


def kernel(
    q_hbm, k_hbm, v_hbm, picks_hbm, w_hbm, out_ref,
    picks, kv, qbuf, vraw, pout, sout, pin, sin, wbuf, att, top, total, acc,
    x_sem, local_sem, kv_send, kv_recv, q_send, q_recv, p_send, p_recv, h_send, h_recv,
):
    ctx = lax.axis_index("ctx")
    head = lax.axis_index("head")
    x = ctx // 32
    z = (ctx % 32) // 4
    y = ctx % 4
    half = z // 4
    low = z % 4
    span = 2 * x + half
    pair_z = z + 1 - 2 * (z % 2)
    across = z - low + (low + 2) % 4
    mate_z = [z, across, 7 - z, 7 - across]
    other = 1 - head

    def device(to_x, to_z, to_y):
        return (to_x * 32 + to_z * 4 + to_y, head)

    def remote(src, dst, send, recv, to):
        return pltpu.make_async_remote_copy(
            src_ref=src, dst_ref=dst, send_sem=send, recv_sem=recv, device_id=to, device_id_type=MESH
        )

    mine = [
        pltpu.make_async_copy(v_hbm, vraw, local_sem.at[0]),
        pltpu.make_async_copy(k_hbm, kv.at[0, y, pl.ds(0, BLK)], local_sem.at[1]),
        pltpu.make_async_copy(q_hbm, qbuf.at[0], local_sem.at[2]),
        pltpu.make_async_copy(
            w_hbm.at[:, pl.ds(pl.multiple_of(head * COLS, COLS), COLS)], wbuf.at[0], local_sem.at[3]
        ),
        pltpu.make_async_copy(picks_hbm, picks, local_sem.at[4]),
    ]
    row_peers = [(d, device(x, z, (y + d) % YN)) for d in range(1, YN)]
    pair_peers = [(d, device(x, pair_z, (y + d) % YN)) for d in range(YN)]
    x_peers = [device((x + d) % XN, z, y) for d in range(1, XN)]
    greeted = [to for _, to in row_peers + pair_peers]
    greeted += [device(x, mate_z[k], y) for k in range(1, MATES)] + x_peers + [(ctx, other)]
    barrier = pltpu.get_barrier_semaphore()
    for to in greeted:
        pl.semaphore_signal(barrier, inc=1, device_id=to, device_id_type=MESH)
    for copy in mine:
        copy.start()

    @pl.when(low >= 2)
    def _():
        qbuf[1] = jnp.zeros((BLK, BLK), jnp.bfloat16)

    mine[0].wait()
    kv[0, y, BLK:] = vraw[...].T
    mine[1].wait()
    mine[2].wait()
    pl.semaphore_wait(barrier, len(greeted))
    for to in x_peers:
        pl.semaphore_signal(x_sem, inc=1, device_id=to, device_id_type=MESH)

    def row_copy(d, to):
        return remote(kv.at[0, y], kv.at[0, y], kv_send.at[0, d], kv_recv.at[0, d], to)

    def pair_copy(d, to):
        return remote(kv.at[0, y], kv.at[1, y], kv_send.at[1, d], kv_recv.at[1, d], to)

    def q_copy(dx, k):
        slot = dx * MATES + k
        to = device((x + XN - dx) % XN, mate_z[k], y)
        return remote(qbuf.at[0], qbuf.at[slot], q_send.at[slot], q_recv.at[slot], to)

    def p_copies(slot, to):
        return [
            remote(pout.at[slot], pin.at[slot], p_send.at[slot, 0], p_recv.at[slot, 0], to),
            remote(sout.at[slot], sin.at[slot], p_send.at[slot, 1], p_recv.at[slot, 1], to),
        ]

    def visits(dx, k):
        if dx:
            return x >= dx
        return low >= 2 if k == 1 else half == 1

    def hosts(dx, k):
        if dx:
            return x + dx < XN
        return low < 2 if k == 1 else half == 0

    w_copy = remote(
        w_hbm.at[:, pl.ds(pl.multiple_of(other * COLS, COLS), COLS)],
        wbuf.at[1], h_send.at[0], h_recv.at[0], (ctx, other),
    )
    att_copy = remote(att.at[0], att.at[1], h_send.at[1], h_recv.at[1], (ctx, other))

    for d, to in row_peers:
        row_copy(d, to).start()
    for d, to in pair_peers:
        pair_copy(d, to).start()
    near = [(dx, 0) for dx in range(1, XN)] + [(0, k) for k in range(1, MATES)]
    far = [(dx, k) for dx in range(1, XN) for k in range(1, MATES)]
    for dx, k in near:
        @pl.when(visits(dx, k))
        def _():
            q_copy(dx, k).start()
    pl.semaphore_wait(x_sem, len(x_peers))
    for dx, k in far:
        @pl.when(visits(dx, k))
        def _():
            q_copy(dx, k).start()
    w_copy.start()

    def attend(i, p, masked):
        queries = qbuf[pl.ds(2 * p, 2)].reshape(2 * BLK, BLK)
        keys = kv[i, :, 0:BLK].reshape(CHUNK, BLK)
        scores = lax.dot_general(
            keys, queries, (((1,), (1,)), ((), ())), preferred_element_type=jnp.float32
        )
        if masked:
            key = lax.broadcasted_iota(jnp.int32, (CHUNK, 2 * BLK), 0)
            token = lax.broadcasted_iota(jnp.int32, (CHUNK, 2 * BLK), 1)
            if i == 0:
                last = y * BLK + token
            else:
                last = jnp.where(pair_z < z, CHUNK, -1)
            allowed = (token >= BLK) | (key <= last)
            scores = jnp.where(allowed, scores, NEGATIVE)
        high = jnp.max(scores, axis=0, keepdims=True)
        if i:
            high = jnp.maximum(high, top[p])
        weights = jnp.exp2((scores - high) * RATE)
        part = jnp.sum(weights, axis=0, keepdims=True)
        values = jnp.concatenate([kv[i, b, BLK:] for b in range(YN)], axis=1)
        numer = jnp.dot(values, weights.astype(jnp.bfloat16), preferred_element_type=jnp.float32)
        if i:
            fade = jnp.exp2((top[p] - high) * RATE)
            part = part + total[p] * fade
            numer = numer + acc[p] * fade
        top[p] = high
        total[p] = part
        acc[p] = numer

    def give_back(p, side, slot, to):
        lanes = slice(side * BLK, (side + 1) * BLK)
        part = total[p, :, lanes]
        pout[slot] = (acc[p, :, lanes] / part).astype(jnp.bfloat16)
        sout[slot, 0:4] = jnp.broadcast_to(top[p, :, lanes], (4, BLK))
        sout[slot, 4:8] = jnp.broadcast_to(part, (4, BLK))
        for copy in p_copies(slot, to):
            copy.start()

    first, ends = 1 + half, 2 * (XN - x)

    def compute(i):
        def body(n, carry):
            p = ends - 1 - n
            attend(i, p, False)
            if i:
                for side in range(2):
                    straight = mate_z[side]
                    to_z = straight + (p % 2) * (7 - 2 * straight)
                    give_back(p, side, 2 * p + side, device(x + p // 2, to_z, y))
            return carry

        lax.fori_loop(0, ends - first, body, 0)
        attend(i, 0, True)
        if i:
            @pl.when(low < 2)
            def _():
                give_back(0, 1, 1, device(x, across, y))

    for d, to in row_peers:
        row_copy(d, to).wait_recv()
    for dx, k in near + far:
        @pl.when(hosts(dx, k))
        def _():
            q_copy(dx, k).wait_recv()
    compute(0)
    for d, to in pair_peers:
        pair_copy(d, to).wait_recv()
    compute(1)

    mine[4].wait()
    first_pick, second_pick = picks[0, 0, ctx], picks[0, 1, ctx]
    for dx, k in [(0, 1), (0, 2), (0, 3)] + [(dx, k) for dx in (1, 3, 2) for k in range(MATES)]:
        @pl.when(visits(dx, k))
        def _():
            slot = dx * MATES + k
            for copy in p_copies(slot, (ctx, head)):
                copy.wait_recv()
            theirs = sin[slot, 0:1]
            if (dx, k) != (0, 1):
                which = 2 * (x - dx) + (half if k < 2 else 1 - half)
                picked = (first_pick == which) | (second_pick == which)
                theirs = jnp.where(picked, theirs, NEGATIVE)
            ours = top[0, :, 0:BLK]
            high = jnp.maximum(ours, theirs)
            fade = jnp.exp2((ours - high) * RATE)
            share = sin[slot, 4:5] * jnp.exp2((theirs - high) * RATE)
            top[0, :, 0:BLK] = high
            total[0, :, 0:BLK] = total[0, :, 0:BLK] * fade + share
            acc[0, :, 0:BLK] = acc[0, :, 0:BLK] * fade + pin[slot].astype(jnp.float32) * share

    att[0] = (acc[0, :, 0:BLK] / total[0, :, 0:BLK]).T.astype(jnp.bfloat16)
    att_copy.start()
    mine[3].wait()
    w_copy.wait_recv()
    att_copy.wait_recv()
    attended = jnp.concatenate([att[0], att[1]], axis=1)
    wide = 512

    def project(n, carry):
        columns = pl.ds(pl.multiple_of(n * wide, wide), wide)
        weight = wbuf[:, :, columns].reshape(2 * BLK, wide)
        out_ref[:, columns] = jnp.dot(attended, weight, preferred_element_type=jnp.float32).astype(jnp.bfloat16)
        return carry

    lax.fori_loop(0, COLS // wide, project, 0)

    for d, to in row_peers:
        row_copy(d, to).wait_send()
    for d, to in pair_peers:
        pair_copy(d, to).wait_send()
    for dx, k in near + far:
        @pl.when(visits(dx, k))
        def _():
            q_copy(dx, k).wait_send()

        @pl.when(hosts(dx, k))
        def _():
            for copy in p_copies(dx * MATES + k, device((x + dx) % XN, mate_z[k], y)):
                copy.wait_send()
    w_copy.wait_send()
    att_copy.wait_send()


def local(queries, keys, values, picks, out_weight):
    hbm = pl.BlockSpec(memory_space=pltpu.HBM)
    dma = pltpu.SemaphoreType.DMA
    bf16, f32 = jnp.bfloat16, jnp.float32
    return pl.pallas_call(
        kernel,
        out_shape=jax.ShapeDtypeStruct((BLK, COLS), bf16),
        in_specs=[hbm] * 5,
        out_specs=pl.BlockSpec(memory_space=pltpu.VMEM),
        scratch_shapes=[
            pltpu.SMEM((1, 2, BLK), jnp.int32),
            pltpu.VMEM((2, YN, 2 * BLK, BLK), bf16),
            pltpu.VMEM((SLOTS, BLK, BLK), bf16),
            pltpu.VMEM((BLK, BLK), bf16),
            pltpu.VMEM((SLOTS, BLK, BLK), bf16),
            pltpu.VMEM((SLOTS, 8, BLK), f32),
            pltpu.VMEM((SLOTS, BLK, BLK), bf16),
            pltpu.VMEM((SLOTS, 8, BLK), f32),
            pltpu.VMEM((2, BLK, COLS), bf16),
            pltpu.VMEM((2, BLK, BLK), bf16),
            pltpu.VMEM((SLOTS // 2, 1, 2 * BLK), f32),
            pltpu.VMEM((SLOTS // 2, 1, 2 * BLK), f32),
            pltpu.VMEM((SLOTS // 2, BLK, 2 * BLK), f32),
            pltpu.SemaphoreType.REGULAR,
            dma((5,)),
            dma((2, YN)),
            dma((2, YN)),
            dma((SLOTS,)),
            dma((SLOTS,)),
            dma((SLOTS, 2)),
            dma((SLOTS, 2)),
            dma((2,)),
            dma((2,)),
        ],
        compiler_params=pltpu.CompilerParams(
            collective_id=0, has_side_effects=True, vmem_limit_bytes=56 * 1024 * 1024
        ),
        cost_estimate=pl.CostEstimate(flops=2**30, bytes_accessed=2**22, transcendentals=2**21),
    )(queries, keys, values, jnp.swapaxes(picks, 1, 2), out_weight)


def solution(mesh):
    placed = (
        P("ctx", "head"),
        P("ctx", "head"),
        P("ctx", "head"),
        P("head", None, None),
        P("head", None),
    )
    return jax.shard_map(
        local, mesh=mesh, in_specs=placed, out_specs=P("ctx", "head"), check_vma=False
    )
```

```python
import math

import jax
import jax.numpy as jnp
from jax import lax
from jax.experimental import pallas as pl
from jax.experimental.pallas import tpu as pltpu
from jax.sharding import PartitionSpec as P

BLK = 128
XN = 4
YN = 4
MATES = 4
SLOTS = XN * MATES
CHUNK = YN * BLK
COLS = 2048
NEGATIVE = -1e30
RATE = math.log2(math.e) / math.sqrt(128.0)
MESH = pl.DeviceIdType.MESH


def kernel(
    q_hbm, k_hbm, v_hbm, picks_hbm, w_hbm, out_ref,
    picks, kv, qbuf, vraw, pout, sout, pin, sin, wbuf, att, top, total, acc,
    x_sem, local_sem, kv_send, kv_recv, q_send, q_recv, p_send, p_recv, h_send, h_recv,
):
    ctx = lax.axis_index("ctx")
    head = lax.axis_index("head")
    x = ctx // 32
    z = (ctx % 32) // 4
    y = ctx % 4
    half = z // 4
    low = z % 4
    span = 2 * x + half
    pair_z = z + 1 - 2 * (z % 2)
    across = z - low + (low + 2) % 4
    mate_z = [z, across, 7 - z, 7 - across]
    other = 1 - head

    def device(to_x, to_z, to_y):
        return (to_x * 32 + to_z * 4 + to_y, head)

    def remote(src, dst, send, recv, to):
        return pltpu.make_async_remote_copy(
            src_ref=src, dst_ref=dst, send_sem=send, recv_sem=recv, device_id=to, device_id_type=MESH
        )

    mine = [
        pltpu.make_async_copy(v_hbm, vraw, local_sem.at[0]),
        pltpu.make_async_copy(k_hbm, kv.at[0, y, pl.ds(0, BLK)], local_sem.at[1]),
        pltpu.make_async_copy(q_hbm, qbuf.at[0], local_sem.at[2]),
        pltpu.make_async_copy(
            w_hbm.at[:, pl.ds(pl.multiple_of(head * COLS, COLS), COLS)], wbuf.at[0], local_sem.at[3]
        ),
        pltpu.make_async_copy(picks_hbm, picks, local_sem.at[4]),
    ]
    row_peers = [(d, device(x, z, (y + d) % YN)) for d in range(1, YN)]
    pair_peers = [(d, device(x, pair_z, (y + d) % YN)) for d in range(YN)]
    x_peers = [device((x + d) % XN, z, y) for d in range(1, XN)]
    greeted = [to for _, to in row_peers + pair_peers]
    greeted += [device(x, mate_z[k], y) for k in range(1, MATES)] + x_peers + [(ctx, other)]
    barrier = pltpu.get_barrier_semaphore()
    for to in greeted:
        pl.semaphore_signal(barrier, inc=1, device_id=to, device_id_type=MESH)
    for copy in mine:
        copy.start()

    @pl.when(low >= 2)
    def _():
        qbuf[1] = jnp.zeros((BLK, BLK), jnp.bfloat16)

    @pl.when(half == 1)
    def _():
        qbuf[2:4] = jnp.zeros((2, BLK, BLK), jnp.bfloat16)

    mine[0].wait()
    kv[0, y, BLK:] = vraw[...].T
    mine[1].wait()
    mine[2].wait()
    pl.semaphore_wait(barrier, len(greeted))
    for to in x_peers:
        pl.semaphore_signal(x_sem, inc=1, device_id=to, device_id_type=MESH)

    def row_copy(d, to):
        return remote(kv.at[0, y], kv.at[0, y], kv_send.at[0, d], kv_recv.at[0, d], to)

    def pair_copy(d, to):
        return remote(kv.at[0, y], kv.at[1, y], kv_send.at[1, d], kv_recv.at[1, d], to)

    def q_copy(dx, k):
        slot = dx * MATES + k
        to = device((x + XN - dx) % XN, mate_z[k], y)
        return remote(qbuf.at[0], qbuf.at[slot], q_send.at[slot], q_recv.at[slot], to)

    def p_copies(slot, to):
        return [
            remote(pout.at[slot], pin.at[slot], p_send.at[slot, 0], p_recv.at[slot, 0], to),
            remote(sout.at[slot], sin.at[slot], p_send.at[slot, 1], p_recv.at[slot, 1], to),
        ]

    def visits(dx, k):
        if dx:
            return x >= dx
        return low >= 2 if k == 1 else half == 1

    def hosts(dx, k):
        if dx:
            return x + dx < XN
        return low < 2 if k == 1 else half == 0

    w_copy = remote(
        w_hbm.at[:, pl.ds(pl.multiple_of(other * COLS, COLS), COLS)],
        wbuf.at[1], h_send.at[0], h_recv.at[0], (ctx, other),
    )
    att_copy = remote(att.at[0], att.at[1], h_send.at[1], h_recv.at[1], (ctx, other))

    for d, to in row_peers:
        row_copy(d, to).start()
    for d, to in pair_peers:
        pair_copy(d, to).start()
    near = [(0, k) for k in range(1, MATES)] + [(dx, 0) for dx in (2, 3, 1)]
    far = [(dx, k) for dx in (2, 3, 1) for k in range(1, MATES)]
    for dx, k in near:
        @pl.when(visits(dx, k))
        def _():
            q_copy(dx, k).start()
    pl.semaphore_wait(x_sem, len(x_peers))
    for dx, k in far:
        @pl.when(visits(dx, k))
        def _():
            q_copy(dx, k).start()
    w_copy.start()

    def attend(dx):
        queries = qbuf[pl.ds(dx * MATES, MATES)].reshape(MATES * BLK, BLK)
        keys = jnp.concatenate([kv[i, :, 0:BLK].reshape(CHUNK, BLK) for i in range(2)], axis=0)
        scores = lax.dot_general(
            keys, queries, (((1,), (1,)), ((), ())), preferred_element_type=jnp.float32
        )
        if dx == 0:
            key = lax.broadcasted_iota(jnp.int32, (2 * CHUNK, BLK), 0)
            token = lax.broadcasted_iota(jnp.int32, (2 * CHUNK, BLK), 1)
            last = jnp.where(key < CHUNK, y * BLK + token, jnp.where(pair_z < z, 2 * CHUNK, -1))
            own = jnp.where(key <= last, scores[:, 0:BLK], NEGATIVE)
            scores = jnp.concatenate([own, scores[:, BLK:]], axis=1)
        high = jnp.max(scores, axis=0, keepdims=True)
        weights = jnp.exp2((scores - high) * RATE)
        part = jnp.sum(weights, axis=0, keepdims=True)
        values = jnp.concatenate([kv[i, b, BLK:] for i in range(2) for b in range(YN)], axis=1)
        numer = jnp.dot(values, weights.astype(jnp.bfloat16), preferred_element_type=jnp.float32)
        if dx == 0:
            top[...] = high[:, 0:BLK]
            total[...] = part[:, 0:BLK]
            acc[...] = numer[:, 0:BLK]
        for k in range(MATES):
            if (dx, k) == (0, 0):
                continue
            slot = dx * MATES + k
            lanes = slice(k * BLK, (k + 1) * BLK)
            pout[slot] = (numer[:, lanes] / part[:, lanes]).astype(jnp.bfloat16)
            sout[slot, 0:4] = jnp.broadcast_to(high[:, lanes], (4, BLK))
            sout[slot, 4:8] = jnp.broadcast_to(part[:, lanes], (4, BLK))

    def serve(dx):
        for k in range(MATES):
            if (dx, k) != (0, 0):
                @pl.when(hosts(dx, k))
                def _():
                    q_copy(dx, k).wait_recv()
        attend(dx)
        for k in range(MATES):
            if (dx, k) != (0, 0):
                @pl.when(hosts(dx, k))
                def _():
                    for copy in p_copies(dx * MATES + k, device((x + dx) % XN, mate_z[k], y)):
                        copy.start()

    for d, to in row_peers:
        row_copy(d, to).wait_recv()
    for d, to in pair_peers:
        pair_copy(d, to).wait_recv()
    serve(0)
    for dx in (2, 3, 1):
        @pl.when(x + dx < XN)
        def _():
            serve(dx)

    mine[4].wait()
    first_pick, second_pick = picks[0, 0, ctx], picks[0, 1, ctx]

    def combine(dx, ks):
        slots = [dx * MATES + k for k in ks]
        theirs = []
        for k, slot in zip(ks, slots):
            for copy in p_copies(slot, (ctx, head)):
                copy.wait_recv()
            score = sin[slot, 0:1]
            if (dx, k) != (0, 1):
                which = 2 * (x - dx) + (half if k < 2 else 1 - half)
                score = jnp.where((first_pick == which) | (second_pick == which), score, NEGATIVE)
            theirs.append(score)
        ours = top[...]
        high = ours
        for score in theirs:
            high = jnp.maximum(high, score)
        fade = jnp.exp2((ours - high) * RATE)
        part = total[...] * fade
        numer = acc[...] * fade
        for score, slot in zip(theirs, slots):
            share = sin[slot, 4:5] * jnp.exp2((score - high) * RATE)
            part = part + share
            numer = numer + pin[slot].astype(jnp.float32) * share
        top[...] = high
        total[...] = part
        acc[...] = numer

    for dx, ks in [(0, (1,)), (0, (2, 3)), (2, range(MATES)), (1, range(MATES)), (3, range(MATES))]:
        @pl.when(visits(dx, ks[0]))
        def _():
            combine(dx, ks)

    att[0] = (acc[...] / total[...]).T.astype(jnp.bfloat16)
    att_copy.start()
    mine[3].wait()
    w_copy.wait_recv()
    att_copy.wait_recv()
    attended = jnp.concatenate([att[0], att[1]], axis=1)
    wide = 512

    def project(n, carry):
        columns = pl.ds(pl.multiple_of(n * wide, wide), wide)
        weight = wbuf[:, :, columns].reshape(2 * BLK, wide)
        out_ref[:, columns] = jnp.dot(attended, weight, preferred_element_type=jnp.float32).astype(jnp.bfloat16)
        return carry

    for n in range(COLS // wide):
        project(n, 0)

    for d, to in row_peers:
        row_copy(d, to).wait_send()
    for d, to in pair_peers:
        pair_copy(d, to).wait_send()
    for dx, k in near + far:
        @pl.when(visits(dx, k))
        def _():
            q_copy(dx, k).wait_send()

        @pl.when(hosts(dx, k))
        def _():
            for copy in p_copies(dx * MATES + k, device((x + dx) % XN, mate_z[k], y)):
                copy.wait_send()
    w_copy.wait_send()
    att_copy.wait_send()


def local(queries, keys, values, picks, out_weight):
    hbm = pl.BlockSpec(memory_space=pltpu.HBM)
    dma = pltpu.SemaphoreType.DMA
    bf16, f32 = jnp.bfloat16, jnp.float32
    return pl.pallas_call(
        kernel,
        out_shape=jax.ShapeDtypeStruct((BLK, COLS), bf16),
        in_specs=[hbm] * 5,
        out_specs=pl.BlockSpec(memory_space=pltpu.VMEM),
        scratch_shapes=[
            pltpu.SMEM((1, 2, BLK), jnp.int32),
            pltpu.VMEM((2, YN, 2 * BLK, BLK), bf16),
            pltpu.VMEM((SLOTS, BLK, BLK), bf16),
            pltpu.VMEM((BLK, BLK), bf16),
            pltpu.VMEM((SLOTS, BLK, BLK), bf16),
            pltpu.VMEM((SLOTS, 8, BLK), f32),
            pltpu.VMEM((SLOTS, BLK, BLK), bf16),
            pltpu.VMEM((SLOTS, 8, BLK), f32),
            pltpu.VMEM((2, BLK, COLS), bf16),
            pltpu.VMEM((2, BLK, BLK), bf16),
            pltpu.VMEM((1, BLK), f32),
            pltpu.VMEM((1, BLK), f32),
            pltpu.VMEM((BLK, BLK), f32),
            pltpu.SemaphoreType.REGULAR,
            dma((5,)),
            dma((2, YN)),
            dma((2, YN)),
            dma((SLOTS,)),
            dma((SLOTS,)),
            dma((SLOTS, 2)),
            dma((SLOTS, 2)),
            dma((2,)),
            dma((2,)),
        ],
        compiler_params=pltpu.CompilerParams(
            collective_id=0, has_side_effects=True, vmem_limit_bytes=56 * 1024 * 1024
        ),
        cost_estimate=pl.CostEstimate(flops=2**30, bytes_accessed=2**22, transcendentals=2**21),
    )(queries, keys, values, jnp.swapaxes(picks, 1, 2), out_weight)


def solution(mesh):
    placed = (
        P("ctx", "head"),
        P("ctx", "head"),
        P("ctx", "head"),
        P("head", None, None),
        P("head", None),
    )
    return jax.shard_map(
        local, mesh=mesh, in_specs=placed, out_specs=P("ctx", "head"), check_vma=False
    )
```

```python
import math

import jax
import jax.numpy as jnp
from jax import lax
from jax.experimental import pallas as pl
from jax.experimental.pallas import tpu as pltpu
from jax.sharding import PartitionSpec as P

BLK = 128
XN = 4
YN = 4
MATES = 4
SLOTS = XN * MATES
CHUNK = YN * BLK
COLS = 2048
NEGATIVE = -1e30
RATE = math.log2(math.e) / math.sqrt(128.0)
MESH = pl.DeviceIdType.MESH


def kernel(
    q_hbm, k_hbm, v_hbm, picks_hbm, w_hbm, out_ref,
    picks, kv, qbuf, vraw, pout, sout, pin, sin, wbuf, att, top, total, acc,
    x_sem, local_sem, kv_send, kv_recv, q_send, q_recv, p_send, p_recv, h_send, h_recv,
):
    ctx = lax.axis_index("ctx")
    head = lax.axis_index("head")
    x = ctx // 32
    z = (ctx % 32) // 4
    y = ctx % 4
    half = z // 4
    low = z % 4
    span = 2 * x + half
    pair_z = z + 1 - 2 * (z % 2)
    across = z - low + (low + 2) % 4
    mate_z = [z, across, 7 - z, 7 - across]
    other = 1 - head

    def device(to_x, to_z, to_y):
        return (to_x * 32 + to_z * 4 + to_y, head)

    def remote(src, dst, send, recv, to):
        return pltpu.make_async_remote_copy(
            src_ref=src, dst_ref=dst, send_sem=send, recv_sem=recv, device_id=to, device_id_type=MESH
        )

    mine = [
        pltpu.make_async_copy(v_hbm, vraw, local_sem.at[0]),
        pltpu.make_async_copy(k_hbm, kv.at[0, y, pl.ds(0, BLK)], local_sem.at[1]),
        pltpu.make_async_copy(q_hbm, qbuf.at[0], local_sem.at[2]),
        pltpu.make_async_copy(
            w_hbm.at[:, pl.ds(pl.multiple_of(head * COLS, COLS), COLS)], wbuf.at[0], local_sem.at[3]
        ),
        pltpu.make_async_copy(picks_hbm, picks, local_sem.at[4]),
    ]
    row_peers = [(d, device(x, z, (y + d) % YN)) for d in range(1, YN)]
    pair_peer = device(x, pair_z, y)
    x_peers = [device((x + d) % XN, z, y) for d in range(1, XN)]
    greeted = [to for _, to in row_peers] + [pair_peer]
    greeted += [device(x, mate_z[k], y) for k in range(1, MATES)] + x_peers + [(ctx, other)]
    barrier = pltpu.get_barrier_semaphore()
    for to in greeted:
        pl.semaphore_signal(barrier, inc=1, device_id=to, device_id_type=MESH)
    for copy in mine:
        copy.start()

    @pl.when(low >= 2)
    def _():
        qbuf[1] = jnp.zeros((BLK, BLK), jnp.bfloat16)

    @pl.when(half == 1)
    def _():
        qbuf[2:4] = jnp.zeros((2, BLK, BLK), jnp.bfloat16)

    mine[0].wait()
    kv[0, y, BLK:] = vraw[...].T
    mine[1].wait()
    mine[2].wait()
    pl.semaphore_wait(barrier, len(greeted))
    for to in x_peers:
        pl.semaphore_signal(x_sem, inc=1, device_id=to, device_id_type=MESH)

    def row_copy(i, d, to):
        return remote(kv.at[i, y], kv.at[i, y], kv_send.at[i, d], kv_recv.at[i, d], to)

    pair_copy = remote(kv.at[0, y], kv.at[1, y], kv_send.at[1, 0], kv_recv.at[1, 0], pair_peer)

    def q_copy(dx, k):
        slot = dx * MATES + k
        to = device((x + XN - dx) % XN, mate_z[k], y)
        return remote(qbuf.at[0], qbuf.at[slot], q_send.at[slot], q_recv.at[slot], to)

    def p_copies(slot, to):
        return [
            remote(pout.at[slot], pin.at[slot], p_send.at[slot, 0], p_recv.at[slot, 0], to),
            remote(sout.at[slot], sin.at[slot], p_send.at[slot, 1], p_recv.at[slot, 1], to),
        ]

    def visits(dx, k):
        if dx:
            return x >= dx
        return low >= 2 if k == 1 else half == 1

    def hosts(dx, k):
        if dx:
            return x + dx < XN
        return low < 2 if k == 1 else half == 0

    w_copy = remote(
        w_hbm.at[:, pl.ds(pl.multiple_of(other * COLS, COLS), COLS)],
        wbuf.at[1], h_send.at[0], h_recv.at[0], (ctx, other),
    )
    att_copy = remote(att.at[0], att.at[1], h_send.at[1], h_recv.at[1], (ctx, other))

    pair_copy.start()
    for d, to in row_peers:
        row_copy(0, d, to).start()
    near = [(0, k) for k in range(1, MATES)] + [(dx, 0) for dx in (2, 3, 1)]
    far = [(dx, k) for dx in (2, 3, 1) for k in range(1, MATES)]
    for dx, k in near:
        @pl.when(visits(dx, k))
        def _():
            q_copy(dx, k).start()
    pl.semaphore_wait(x_sem, len(x_peers))
    for dx, k in far:
        @pl.when(visits(dx, k))
        def _():
            q_copy(dx, k).start()
    w_copy.start()
    pair_copy.wait_recv()
    for d, to in row_peers:
        row_copy(1, d, to).start()

    def attend(dx):
        queries = qbuf[pl.ds(dx * MATES, MATES)].reshape(MATES * BLK, BLK)
        keys = jnp.concatenate([kv[i, :, 0:BLK].reshape(CHUNK, BLK) for i in range(2)], axis=0)
        scores = lax.dot_general(
            keys, queries, (((1,), (1,)), ((), ())), preferred_element_type=jnp.float32
        )
        if dx == 0:
            key = lax.broadcasted_iota(jnp.int32, (2 * CHUNK, BLK), 0)
            token = lax.broadcasted_iota(jnp.int32, (2 * CHUNK, BLK), 1)
            last = jnp.where(key < CHUNK, y * BLK + token, jnp.where(pair_z < z, 2 * CHUNK, -1))
            own = jnp.where(key <= last, scores[:, 0:BLK], NEGATIVE)
            scores = jnp.concatenate([own, scores[:, BLK:]], axis=1)
        high = jnp.max(scores, axis=0, keepdims=True)
        weights = jnp.exp2((scores - high) * RATE)
        part = jnp.sum(weights, axis=0, keepdims=True)
        values = jnp.concatenate([kv[i, b, BLK:] for i in range(2) for b in range(YN)], axis=1)
        numer = jnp.dot(values, weights.astype(jnp.bfloat16), preferred_element_type=jnp.float32)
        if dx == 0:
            top[...] = high[:, 0:BLK]
            total[...] = part[:, 0:BLK]
            acc[...] = numer[:, 0:BLK]
        for k in range(MATES):
            if (dx, k) == (0, 0):
                continue
            slot = dx * MATES + k
            lanes = slice(k * BLK, (k + 1) * BLK)
            pout[slot] = (numer[:, lanes] / part[:, lanes]).astype(jnp.bfloat16)
            sout[slot, 0:4] = jnp.broadcast_to(high[:, lanes], (4, BLK))
            sout[slot, 4:8] = jnp.broadcast_to(part[:, lanes], (4, BLK))

    def serve(dx):
        for k in range(MATES):
            if (dx, k) != (0, 0):
                @pl.when(hosts(dx, k))
                def _():
                    q_copy(dx, k).wait_recv()
        attend(dx)
        for k in range(MATES):
            if (dx, k) != (0, 0):
                @pl.when(hosts(dx, k))
                def _():
                    for copy in p_copies(dx * MATES + k, device((x + dx) % XN, mate_z[k], y)):
                        copy.start()

    for i in range(2):
        for d, to in row_peers:
            row_copy(i, d, to).wait_recv()
    serve(0)
    for dx in (2, 3, 1):
        @pl.when(x + dx < XN)
        def _():
            serve(dx)

    mine[4].wait()
    first_pick, second_pick = picks[0, 0, ctx], picks[0, 1, ctx]

    def combine(dx, ks):
        slots = [dx * MATES + k for k in ks]
        theirs = []
        for k, slot in zip(ks, slots):
            for copy in p_copies(slot, (ctx, head)):
                copy.wait_recv()
            score = sin[slot, 0:1]
            if (dx, k) != (0, 1):
                which = 2 * (x - dx) + (half if k < 2 else 1 - half)
                score = jnp.where((first_pick == which) | (second_pick == which), score, NEGATIVE)
            theirs.append(score)
        ours = top[...]
        high = ours
        for score in theirs:
            high = jnp.maximum(high, score)
        fade = jnp.exp2((ours - high) * RATE)
        part = total[...] * fade
        numer = acc[...] * fade
        for score, slot in zip(theirs, slots):
            share = sin[slot, 4:5] * jnp.exp2((score - high) * RATE)
            part = part + share
            numer = numer + pin[slot].astype(jnp.float32) * share
        top[...] = high
        total[...] = part
        acc[...] = numer

    for dx, ks in [(0, (1,)), (0, (2, 3)), (2, range(MATES)), (1, range(MATES)), (3, range(MATES))]:
        @pl.when(visits(dx, ks[0]))
        def _():
            combine(dx, ks)

    att[0] = (acc[...] / total[...]).T.astype(jnp.bfloat16)
    att_copy.start()
    mine[3].wait()
    w_copy.wait_recv()
    att_copy.wait_recv()
    attended = jnp.concatenate([att[0], att[1]], axis=1)
    wide = 512

    def project(n, carry):
        columns = pl.ds(pl.multiple_of(n * wide, wide), wide)
        weight = wbuf[:, :, columns].reshape(2 * BLK, wide)
        out_ref[:, columns] = jnp.dot(attended, weight, preferred_element_type=jnp.float32).astype(jnp.bfloat16)
        return carry

    for n in range(COLS // wide):
        project(n, 0)

    pair_copy.wait_send()
    for i in range(2):
        for d, to in row_peers:
            row_copy(i, d, to).wait_send()
    for dx, k in near + far:
        @pl.when(visits(dx, k))
        def _():
            q_copy(dx, k).wait_send()

        @pl.when(hosts(dx, k))
        def _():
            for copy in p_copies(dx * MATES + k, device((x + dx) % XN, mate_z[k], y)):
                copy.wait_send()
    w_copy.wait_send()
    att_copy.wait_send()


def local(queries, keys, values, picks, out_weight):
    hbm = pl.BlockSpec(memory_space=pltpu.HBM)
    dma = pltpu.SemaphoreType.DMA
    bf16, f32 = jnp.bfloat16, jnp.float32
    return pl.pallas_call(
        kernel,
        out_shape=jax.ShapeDtypeStruct((BLK, COLS), bf16),
        in_specs=[hbm] * 5,
        out_specs=pl.BlockSpec(memory_space=pltpu.VMEM),
        scratch_shapes=[
            pltpu.SMEM((1, 2, BLK), jnp.int32),
            pltpu.VMEM((2, YN, 2 * BLK, BLK), bf16),
            pltpu.VMEM((SLOTS, BLK, BLK), bf16),
            pltpu.VMEM((BLK, BLK), bf16),
            pltpu.VMEM((SLOTS, BLK, BLK), bf16),
            pltpu.VMEM((SLOTS, 8, BLK), f32),
            pltpu.VMEM((SLOTS, BLK, BLK), bf16),
            pltpu.VMEM((SLOTS, 8, BLK), f32),
            pltpu.VMEM((2, BLK, COLS), bf16),
            pltpu.VMEM((2, BLK, BLK), bf16),
            pltpu.VMEM((1, BLK), f32),
            pltpu.VMEM((1, BLK), f32),
            pltpu.VMEM((BLK, BLK), f32),
            pltpu.SemaphoreType.REGULAR,
            dma((5,)),
            dma((2, YN)),
            dma((2, YN)),
            dma((SLOTS,)),
            dma((SLOTS,)),
            dma((SLOTS, 2)),
            dma((SLOTS, 2)),
            dma((2,)),
            dma((2,)),
        ],
        compiler_params=pltpu.CompilerParams(
            collective_id=0, has_side_effects=True, vmem_limit_bytes=56 * 1024 * 1024
        ),
        cost_estimate=pl.CostEstimate(flops=2**30, bytes_accessed=2**22, transcendentals=2**21),
    )(queries, keys, values, jnp.swapaxes(picks, 1, 2), out_weight)


def solution(mesh):
    placed = (
        P("ctx", "head"),
        P("ctx", "head"),
        P("ctx", "head"),
        P("head", None, None),
        P("head", None),
    )
    return jax.shard_map(
        local, mesh=mesh, in_specs=placed, out_specs=P("ctx", "head"), check_vma=False
    )
```

```python
import math

import jax
import jax.numpy as jnp
from jax import lax
from jax.experimental import pallas as pl
from jax.experimental.pallas import tpu as pltpu
from jax.sharding import PartitionSpec as P

BLK = 128
XN = 4
YN = 4
MATES = 4
SLOTS = XN * MATES
CHUNK = YN * BLK
COLS = 2048
NEGATIVE = -1e30
RATE = math.log2(math.e) / math.sqrt(128.0)
MESH = pl.DeviceIdType.MESH


def kernel(
    q_hbm, k_hbm, v_hbm, picks_hbm, w_hbm, out_ref,
    picks, kv, qbuf, vraw, pout, sout, pin, sin, wbuf, att, top, total, acc,
    x_sem, local_sem, kv_send, kv_recv, q_send, q_recv, p_send, p_recv, h_send, h_recv,
):
    ctx = lax.axis_index("ctx")
    head = lax.axis_index("head")
    x = ctx // 32
    z = (ctx % 32) // 4
    y = ctx % 4
    half = z // 4
    low = z % 4
    span = 2 * x + half
    pair_z = z + 1 - 2 * (z % 2)
    across = z - low + (low + 2) % 4
    mate_z = [z, across, 7 - z, 7 - across]
    other = 1 - head

    def device(to_x, to_z, to_y):
        return (to_x * 32 + to_z * 4 + to_y, head)

    def remote(src, dst, send, recv, to):
        return pltpu.make_async_remote_copy(
            src_ref=src, dst_ref=dst, send_sem=send, recv_sem=recv, device_id=to, device_id_type=MESH
        )

    mine = [
        pltpu.make_async_copy(v_hbm, vraw, local_sem.at[0]),
        pltpu.make_async_copy(k_hbm, kv.at[0, y, pl.ds(0, BLK)], local_sem.at[1]),
        pltpu.make_async_copy(q_hbm, qbuf.at[0], local_sem.at[2]),
        pltpu.make_async_copy(
            w_hbm.at[:, pl.ds(pl.multiple_of(head * COLS, COLS), COLS)], wbuf.at[0], local_sem.at[3]
        ),
        pltpu.make_async_copy(picks_hbm, picks, local_sem.at[4]),
    ]
    row_peers = [(d, device(x, z, (y + d) % YN)) for d in range(1, YN)]
    pair_peer = device(x, pair_z, y)
    x_peers = [device((x + d) % XN, z, y) for d in range(1, XN)]
    greeted = [to for _, to in row_peers] + [pair_peer]
    greeted += [device(x, mate_z[k], y) for k in range(1, MATES)] + x_peers + [(ctx, other)]
    barrier = pltpu.get_barrier_semaphore()
    for to in greeted:
        pl.semaphore_signal(barrier, inc=1, device_id=to, device_id_type=MESH)
    for copy in mine:
        copy.start()

    @pl.when(low >= 2)
    def _():
        qbuf[1] = jnp.zeros((BLK, BLK), jnp.bfloat16)

    @pl.when(half == 1)
    def _():
        qbuf[2:4] = jnp.zeros((2, BLK, BLK), jnp.bfloat16)

    mine[0].wait()
    kv[0, y, BLK:] = vraw[...].T
    mine[1].wait()
    mine[2].wait()
    pl.semaphore_wait(barrier, len(greeted))
    for to in x_peers:
        pl.semaphore_signal(x_sem, inc=1, device_id=to, device_id_type=MESH)

    def row_copy(i, d, to):
        return remote(kv.at[i, y], kv.at[i, y], kv_send.at[i, d], kv_recv.at[i, d], to)

    pair_copy = remote(kv.at[0, y], kv.at[1, y], kv_send.at[1, 0], kv_recv.at[1, 0], pair_peer)

    def q_copy(dx, k):
        slot = dx * MATES + k
        to = device((x + XN - dx) % XN, mate_z[k], y)
        return remote(qbuf.at[0], qbuf.at[slot], q_send.at[slot], q_recv.at[slot], to)

    def p_copies(slot, to):
        return [
            remote(pout.at[slot], pin.at[slot], p_send.at[slot, 0], p_recv.at[slot, 0], to),
            remote(sout.at[slot], sin.at[slot], p_send.at[slot, 1], p_recv.at[slot, 1], to),
        ]

    def visits(dx, k):
        if dx:
            return x >= dx
        return low >= 2 if k == 1 else half == 1

    def hosts(dx, k):
        if dx:
            return x + dx < XN
        return low < 2 if k == 1 else half == 0

    w_copy = remote(
        w_hbm.at[:, pl.ds(pl.multiple_of(other * COLS, COLS), COLS)],
        wbuf.at[1], h_send.at[0], h_recv.at[0], (ctx, other),
    )
    att_copy = remote(att.at[0], att.at[1], h_send.at[1], h_recv.at[1], (ctx, other))

    pair_copy.start()
    for d, to in row_peers:
        row_copy(0, d, to).start()
    near = [(dx, 0) for dx in (2, 3, 1)] + [(0, k) for k in (3, 2, 1)]
    far = [(dx, k) for k in (3, 2, 1) for dx in (2, 3, 1)]
    for dx, k in near:
        @pl.when(visits(dx, k))
        def _():
            q_copy(dx, k).start()
    pl.semaphore_wait(x_sem, len(x_peers))
    for dx, k in far:
        @pl.when(visits(dx, k))
        def _():
            q_copy(dx, k).start()
    w_copy.start()
    pair_copy.wait_recv()
    for d, to in row_peers:
        row_copy(1, d, to).start()

    def attend(dx):
        queries = qbuf[pl.ds(dx * MATES, MATES)].reshape(MATES * BLK, BLK)
        keys = jnp.concatenate([kv[i, :, 0:BLK].reshape(CHUNK, BLK) for i in range(2)], axis=0)
        scores = lax.dot_general(
            keys, queries, (((1,), (1,)), ((), ())), preferred_element_type=jnp.float32
        )
        if dx == 0:
            key = lax.broadcasted_iota(jnp.int32, (2 * CHUNK, BLK), 0)
            token = lax.broadcasted_iota(jnp.int32, (2 * CHUNK, BLK), 1)
            last = jnp.where(key < CHUNK, y * BLK + token, jnp.where(pair_z < z, 2 * CHUNK, -1))
            own = jnp.where(key <= last, scores[:, 0:BLK], NEGATIVE)
            scores = jnp.concatenate([own, scores[:, BLK:]], axis=1)
        high = jnp.max(scores, axis=0, keepdims=True)
        weights = jnp.exp2((scores - high) * RATE)
        part = jnp.sum(weights, axis=0, keepdims=True)
        values = jnp.concatenate([kv[i, b, BLK:] for i in range(2) for b in range(YN)], axis=1)
        numer = jnp.dot(values, weights.astype(jnp.bfloat16), preferred_element_type=jnp.float32)
        if dx == 0:
            top[...] = high[:, 0:BLK]
            total[...] = part[:, 0:BLK]
            acc[...] = numer[:, 0:BLK]
        for k in range(MATES):
            if (dx, k) == (0, 0):
                continue
            slot = dx * MATES + k
            lanes = slice(k * BLK, (k + 1) * BLK)
            pout[slot] = (numer[:, lanes] / part[:, lanes]).astype(jnp.bfloat16)
            sout[slot, 0:4] = jnp.broadcast_to(high[:, lanes], (4, BLK))
            sout[slot, 4:8] = jnp.broadcast_to(part[:, lanes], (4, BLK))

    def serve(dx):
        for k in range(MATES):
            if (dx, k) != (0, 0):
                @pl.when(hosts(dx, k))
                def _():
                    q_copy(dx, k).wait_recv()
        attend(dx)
        for k in range(MATES):
            if (dx, k) != (0, 0):
                @pl.when(hosts(dx, k))
                def _():
                    for copy in p_copies(dx * MATES + k, device((x + dx) % XN, mate_z[k], y)):
                        copy.start()

    for i in range(2):
        for d, to in row_peers:
            row_copy(i, d, to).wait_recv()
    for dx in (1, 2, 3):
        @pl.when(x + dx < XN)
        def _():
            serve(dx)
    serve(0)

    mine[4].wait()
    first_pick, second_pick = picks[0, 0, ctx], picks[0, 1, ctx]

    def combine(dx, ks):
        slots = [dx * MATES + k for k in ks]
        theirs = []
        for k, slot in zip(ks, slots):
            for copy in p_copies(slot, (ctx, head)):
                copy.wait_recv()
            score = sin[slot, 0:1]
            if (dx, k) != (0, 1):
                which = 2 * (x - dx) + (half if k < 2 else 1 - half)
                score = jnp.where((first_pick == which) | (second_pick == which), score, NEGATIVE)
            theirs.append(score)
        ours = top[...]
        high = ours
        for score in theirs:
            high = jnp.maximum(high, score)
        fade = jnp.exp2((ours - high) * RATE)
        part = total[...] * fade
        numer = acc[...] * fade
        for score, slot in zip(theirs, slots):
            share = sin[slot, 4:5] * jnp.exp2((score - high) * RATE)
            part = part + share
            numer = numer + pin[slot].astype(jnp.float32) * share
        top[...] = high
        total[...] = part
        acc[...] = numer

    for dx, ks in [(0, (1,)), (0, (2, 3)), (2, range(MATES)), (1, range(MATES)), (3, range(MATES))]:
        @pl.when(visits(dx, ks[0]))
        def _():
            combine(dx, ks)

    att[0] = (acc[...] / total[...]).T.astype(jnp.bfloat16)
    att_copy.start()
    mine[3].wait()
    w_copy.wait_recv()
    att_copy.wait_recv()
    attended = jnp.concatenate([att[0], att[1]], axis=1)
    wide = 512

    def project(n, carry):
        columns = pl.ds(pl.multiple_of(n * wide, wide), wide)
        weight = wbuf[:, :, columns].reshape(2 * BLK, wide)
        out_ref[:, columns] = jnp.dot(attended, weight, preferred_element_type=jnp.float32).astype(jnp.bfloat16)
        return carry

    for n in range(COLS // wide):
        project(n, 0)

    pair_copy.wait_send()
    for i in range(2):
        for d, to in row_peers:
            row_copy(i, d, to).wait_send()
    for dx, k in near + far:
        @pl.when(visits(dx, k))
        def _():
            q_copy(dx, k).wait_send()

        @pl.when(hosts(dx, k))
        def _():
            for copy in p_copies(dx * MATES + k, device((x + dx) % XN, mate_z[k], y)):
                copy.wait_send()
    w_copy.wait_send()
    att_copy.wait_send()


def local(queries, keys, values, picks, out_weight):
    hbm = pl.BlockSpec(memory_space=pltpu.HBM)
    dma = pltpu.SemaphoreType.DMA
    bf16, f32 = jnp.bfloat16, jnp.float32
    return pl.pallas_call(
        kernel,
        out_shape=pltpu.VMEM((BLK, COLS), bf16),
        in_specs=[hbm] * 5,
        out_specs=pl.BlockSpec(memory_space=pltpu.VMEM),
        scratch_shapes=[
            pltpu.SMEM((1, 2, BLK), jnp.int32),
            pltpu.VMEM((2, YN, 2 * BLK, BLK), bf16),
            pltpu.VMEM((SLOTS, BLK, BLK), bf16),
            pltpu.VMEM((BLK, BLK), bf16),
            pltpu.VMEM((SLOTS, BLK, BLK), bf16),
            pltpu.VMEM((SLOTS, 8, BLK), f32),
            pltpu.VMEM((SLOTS, BLK, BLK), bf16),
            pltpu.VMEM((SLOTS, 8, BLK), f32),
            pltpu.VMEM((2, BLK, COLS), bf16),
            pltpu.VMEM((2, BLK, BLK), bf16),
            pltpu.VMEM((1, BLK), f32),
            pltpu.VMEM((1, BLK), f32),
            pltpu.VMEM((BLK, BLK), f32),
            pltpu.SemaphoreType.REGULAR,
            dma((5,)),
            dma((2, YN)),
            dma((2, YN)),
            dma((SLOTS,)),
            dma((SLOTS,)),
            dma((SLOTS, 2)),
            dma((SLOTS, 2)),
            dma((2,)),
            dma((2,)),
        ],
        compiler_params=pltpu.CompilerParams(
            collective_id=0, has_side_effects=True, vmem_limit_bytes=56 * 1024 * 1024
        ),
        cost_estimate=pl.CostEstimate(flops=2**30, bytes_accessed=2**22, transcendentals=2**21),
    )(queries, keys, values, jnp.swapaxes(picks, 1, 2), out_weight)


def solution(mesh):
    placed = (
        P("ctx", "head"),
        P("ctx", "head"),
        P("ctx", "head"),
        P("head", None, None),
        P("head", None),
    )
    return jax.shard_map(
        local, mesh=mesh, in_specs=placed, out_specs=P("ctx", "head"), check_vma=False
    )
```

```python
import math

import jax
import jax.numpy as jnp
from jax import lax
from jax.experimental import pallas as pl
from jax.experimental.pallas import tpu as pltpu
from jax.sharding import PartitionSpec as P

BLK = 128
XN = 4
YN = 4
ZN = 8
MATES = 4
NEAR = (3, 1, 2)
FORWARD = (2, 3, 1)
SERVE = (3, 1, 2, 0)
SLOTS = MATES * XN
CHUNK = YN * BLK
COLS = 2048
NEGATIVE = -1e30
RATE = math.log2(math.e) / math.sqrt(128.0)
MESH = pl.DeviceIdType.MESH


def kernel(
    q_hbm, k_hbm, v_hbm, picks_hbm, w_hbm, out_ref,
    picks, kv, qbuf, vraw, pout, sout, pin, sin, wbuf, att, top, total, acc,
    local_sem, kv_send, kv_recv, q_send, q_recv, p_send, p_recv, h_send, h_recv,
):
    ctx = lax.axis_index("ctx")
    head = lax.axis_index("head")
    x = ctx // 32
    z = (ctx % 32) // 4
    y = ctx % 4
    span = 2 * x + z // 4
    side = 1 - 2 * (z % 2)
    pair_z = z + side
    host_z = [z, (z + ZN + 2 * side) % ZN, (z + ZN - side) % ZN, (z + ZN - 3 * side) % ZN]
    guest_z = [z, (z + ZN - 2 * side) % ZN, host_z[2], host_z[3]]
    other = 1 - head

    def device(to_x, to_z, to_y):
        return (to_x * 32 + to_z * 4 + to_y, head)

    def remote(src, dst, send, recv, to):
        return pltpu.make_async_remote_copy(
            src_ref=src, dst_ref=dst, send_sem=send, recv_sem=recv, device_id=to, device_id_type=MESH
        )

    mine = [
        pltpu.make_async_copy(v_hbm, vraw, local_sem.at[0]),
        pltpu.make_async_copy(k_hbm, kv.at[0, y, pl.ds(0, BLK)], local_sem.at[1]),
        pltpu.make_async_copy(q_hbm, qbuf.at[0], local_sem.at[2]),
        pltpu.make_async_copy(
            w_hbm.at[:, pl.ds(pl.multiple_of(head * COLS, COLS), COLS)], wbuf.at[0], local_sem.at[3]
        ),
        pltpu.make_async_copy(picks_hbm, picks, local_sem.at[4]),
    ]
    row_peers = [(d, device(x, z, (y + d) % YN)) for d in range(1, YN)]
    pair_peer = device(x, pair_z, y)
    x_peers = [device((x + d) % XN, z, y) for d in range(1, XN)]
    greeted = [to for _, to in row_peers] + [pair_peer]
    greeted += [device(x, to_z, y) for to_z in host_z[1:] + guest_z[1:2]] + x_peers + [(ctx, other)]
    barrier = pltpu.get_barrier_semaphore()
    for to in greeted:
        pl.semaphore_signal(barrier, inc=1, device_id=to, device_id_type=MESH)
    for copy in mine:
        copy.start()

    def visits(dx, k):
        return x >= dx if dx else host_z[k] // 2 < z // 2

    def hosts(dx, k):
        return x + dx < XN if dx else z // 2 < guest_z[k] // 2

    for dx in range(XN):
        for k in range(MATES):
            if dx or k:
                @pl.when(jnp.logical_not(hosts(dx, k) if dx else (x >= 1) | hosts(0, k)))
                def _():
                    qbuf[k * XN + dx] = jnp.zeros((BLK, BLK), jnp.bfloat16)

    mine[0].wait()
    kv[0, y, BLK:] = vraw[...].T
    mine[1].wait()
    mine[2].wait()
    pl.semaphore_wait(barrier, len(greeted))

    def row_copy(i, d, to):
        return remote(kv.at[i, y], kv.at[i, y], kv_send.at[i, d], kv_recv.at[i, d], to)

    pair_copy = remote(kv.at[0, y], kv.at[1, y], kv_send.at[1, 0], kv_recv.at[1, 0], pair_peer)

    def z_copy(k):
        slot = k * XN
        return remote(qbuf.at[0], qbuf.at[slot], q_send.at[slot], q_recv.at[slot], device(x, host_z[k], y))

    def q_copy(dx, k):
        slot = k * XN + dx
        to = device((x + XN - dx) % XN, z, y)
        return remote(qbuf.at[k * XN], qbuf.at[slot], q_send.at[slot], q_recv.at[slot], to)

    def p_copies(slot, to):
        return [
            remote(pout.at[slot], pin.at[slot], p_send.at[slot, 0], p_recv.at[slot, 0], to),
            remote(sout.at[slot], sin.at[slot], p_send.at[slot, 1], p_recv.at[slot, 1], to),
        ]

    w_copy = remote(
        w_hbm.at[:, pl.ds(pl.multiple_of(other * COLS, COLS), COLS)],
        wbuf.at[1], h_send.at[0], h_recv.at[0], (ctx, other),
    )
    att_copy = remote(att.at[0], att.at[1], h_send.at[1], h_recv.at[1], (ctx, other))

    pair_copy.start()
    for d, to in row_peers:
        row_copy(0, d, to).start()
    for k in NEAR:
        @pl.when((x >= 1) | visits(0, k))
        def _():
            z_copy(k).start()
    for dx in FORWARD:
        @pl.when(x >= dx)
        def _():
            q_copy(dx, 0).start()
    w_copy.start()

    def forward(k):
        @pl.when((x >= 1) | hosts(0, k))
        def _():
            z_copy(k).wait_recv()
        for dx in FORWARD:
            @pl.when(x >= dx)
            def _():
                q_copy(dx, k).start()

    pair_copy.wait_recv()
    for d, to in row_peers:
        row_copy(1, d, to).start()
    forward(NEAR[0])
    for k in NEAR[1:]:
        forward(k)

    def attend(k):
        queries = qbuf[k * XN:(k + 1) * XN].reshape(XN * BLK, BLK)
        keys = jnp.concatenate([kv[i, :, 0:BLK].reshape(CHUNK, BLK) for i in range(2)], axis=0)
        scores = lax.dot_general(
            keys, queries, (((1,), (1,)), ((), ())), preferred_element_type=jnp.float32
        )
        if k == 0:
            key = lax.broadcasted_iota(jnp.int32, (2 * CHUNK, BLK), 0)
            token = lax.broadcasted_iota(jnp.int32, (2 * CHUNK, BLK), 1)
            last = jnp.where(key < CHUNK, y * BLK + token, jnp.where(pair_z < z, 2 * CHUNK, -1))
            own = jnp.where(key <= last, scores[:, 0:BLK], NEGATIVE)
            scores = jnp.concatenate([own, scores[:, BLK:]], axis=1)
        high = jnp.max(scores, axis=0, keepdims=True)
        weights = jnp.exp2((scores - high) * RATE)
        part = jnp.sum(weights, axis=0, keepdims=True)
        values = jnp.concatenate([kv[i, b, BLK:] for i in range(2) for b in range(YN)], axis=1)
        numer = jnp.dot(values, weights.astype(jnp.bfloat16), preferred_element_type=jnp.float32)
        if k == 0:
            top[...] = high[:, 0:BLK]
            total[...] = part[:, 0:BLK]
            acc[...] = numer[:, 0:BLK]
        for dx in range(XN):
            if (dx, k) == (0, 0):
                continue
            slot = k * XN + dx
            lanes = slice(dx * BLK, (dx + 1) * BLK)
            pout[slot] = (numer[:, lanes] / part[:, lanes]).astype(jnp.bfloat16)
            sout[slot, 0:1] = high[:, lanes]
            sout[slot, 1:2] = part[:, lanes]

    def serve(k):
        for dx in range(1, XN):
            @pl.when(hosts(dx, k))
            def _():
                q_copy(dx, k).wait_recv()
        attend(k)
        for dx in (2, 3, 1, 0):
            if (dx, k) != (0, 0):
                @pl.when(hosts(dx, k))
                def _():
                    for copy in p_copies(k * XN + dx, device((x + dx) % XN, guest_z[k], y)):
                        copy.start()

    for i in range(2):
        for d, to in row_peers:
            row_copy(i, d, to).wait_recv()
    for k in SERVE:
        @pl.when((x + 1 < XN) | hosts(0, k) if k else x >= 0)
        def _():
            serve(k)

    mine[4].wait()
    first_pick, second_pick = picks[0, 0, ctx], picks[0, 1, ctx]

    def combine(k, dxs):
        slots = [k * XN + dx for dx in dxs]
        theirs = []
        for dx, slot in zip(dxs, slots):
            for copy in p_copies(slot, (ctx, head)):
                copy.wait_recv()
            score = sin[slot, 0:1]
            which = 2 * (x - dx) + host_z[k] // 4
            wanted = (first_pick == which) | (second_pick == which) | (which == span)
            theirs.append(jnp.where(wanted, score, NEGATIVE))
        ours = top[...]
        high = ours
        for score in theirs:
            high = jnp.maximum(high, score)
        fade = jnp.exp2((ours - high) * RATE)
        part = total[...] * fade
        numer = acc[...] * fade
        for score, slot in zip(theirs, slots):
            share = sin[slot, 1:2] * jnp.exp2((score - high) * RATE)
            part = part + share
            numer = numer + pin[slot].astype(jnp.float32) * share
        top[...] = high
        total[...] = part
        acc[...] = numer

    for k in SERVE:
        if k:
            @pl.when(visits(0, k))
            def _():
                combine(k, [0])

        for far_x in range(1, XN):
            @pl.when(x == far_x)
            def _():
                combine(k, range(1, far_x + 1))

    att[0] = (acc[...] / total[...]).T.astype(jnp.bfloat16)
    att_copy.start()
    mine[3].wait()
    w_copy.wait_recv()
    att_copy.wait_recv()
    attended = jnp.concatenate([att[0], att[1]], axis=1)
    wide = 512

    def project(n, carry):
        columns = pl.ds(pl.multiple_of(n * wide, wide), wide)
        weight = wbuf[:, :, columns].reshape(2 * BLK, wide)
        out_ref[:, columns] = jnp.dot(attended, weight, preferred_element_type=jnp.float32).astype(jnp.bfloat16)
        return carry

    for n in range(COLS // wide):
        project(n, 0)

    pair_copy.wait_send()
    for i in range(2):
        for d, to in row_peers:
            row_copy(i, d, to).wait_send()
    for k in range(MATES):
        for dx in range(XN):
            if dx:
                @pl.when(x >= dx)
                def _():
                    q_copy(dx, k).wait_send()
            elif k:
                @pl.when((x >= 1) | visits(0, k))
                def _():
                    z_copy(k).wait_send()
            if dx or k:
                @pl.when(hosts(dx, k))
                def _():
                    for copy in p_copies(k * XN + dx, device((x + dx) % XN, guest_z[k], y)):
                        copy.wait_send()
    w_copy.wait_send()
    att_copy.wait_send()


def local(queries, keys, values, picks, out_weight):
    hbm = pl.BlockSpec(memory_space=pltpu.HBM)
    dma = pltpu.SemaphoreType.DMA
    bf16, f32 = jnp.bfloat16, jnp.float32
    return pl.pallas_call(
        kernel,
        out_shape=pltpu.VMEM((BLK, COLS), bf16),
        in_specs=[hbm] * 5,
        out_specs=pl.BlockSpec(memory_space=pltpu.VMEM),
        scratch_shapes=[
            pltpu.SMEM((1, 2, BLK), jnp.int32),
            pltpu.VMEM((2, YN, 2 * BLK, BLK), bf16),
            pltpu.VMEM((SLOTS, BLK, BLK), bf16),
            pltpu.VMEM((BLK, BLK), bf16),
            pltpu.VMEM((SLOTS, BLK, BLK), bf16),
            pltpu.VMEM((SLOTS, 2, BLK), f32),
            pltpu.VMEM((SLOTS, BLK, BLK), bf16),
            pltpu.VMEM((SLOTS, 2, BLK), f32),
            pltpu.VMEM((2, BLK, COLS), bf16),
            pltpu.VMEM((2, BLK, BLK), bf16),
            pltpu.VMEM((1, BLK), f32),
            pltpu.VMEM((1, BLK), f32),
            pltpu.VMEM((BLK, BLK), f32),
            dma((5,)),
            dma((2, YN)),
            dma((2, YN)),
            dma((SLOTS,)),
            dma((SLOTS,)),
            dma((SLOTS, 2)),
            dma((SLOTS, 2)),
            dma((2,)),
            dma((2,)),
        ],
        compiler_params=pltpu.CompilerParams(
            collective_id=0, has_side_effects=True, vmem_limit_bytes=56 * 1024 * 1024
        ),
        cost_estimate=pl.CostEstimate(flops=2**30, bytes_accessed=2**22, transcendentals=2**21),
    )(queries, keys, values, jnp.swapaxes(picks, 1, 2), out_weight)


def solution(mesh):
    placed = (
        P("ctx", "head"),
        P("ctx", "head"),
        P("ctx", "head"),
        P("head", None, None),
        P("head", None),
    )
    return jax.shard_map(
        local, mesh=mesh, in_specs=placed, out_specs=P("ctx", "head"), check_vma=False
    )
```

```python
import math

import jax
import jax.numpy as jnp
from jax import lax
from jax.experimental import pallas as pl
from jax.experimental.pallas import tpu as pltpu
from jax.sharding import PartitionSpec as P

BLK = 128
XN = 4
YN = 4
ZN = 8
MATES = 4
NEAR = (3, 1, 2)
FORWARD = (3, 2, 1)
SERVE = (3, 1, 2, 0)
SLOTS = MATES * XN
CHUNK = YN * BLK
COLS = 2048
NEGATIVE = -1e30
RATE = math.log2(math.e) / math.sqrt(128.0)
MESH = pl.DeviceIdType.MESH


def kernel(
    q_hbm, k_hbm, v_hbm, picks_hbm, w_hbm, out_ref,
    picks, kv, qbuf, vraw, pout, sout, pin, sin, wbuf, att, term, top, total, acc,
    local_sem, kv_send, kv_recv, q_send, q_recv, p_send, p_recv, h_send, h_recv,
):
    ctx = lax.axis_index("ctx")
    head = lax.axis_index("head")
    x = ctx // 32
    z = (ctx % 32) // 4
    y = ctx % 4
    span = 2 * x + z // 4
    side = 1 - 2 * (z % 2)
    pair_z = z + side
    host_z = [z, (z + ZN + 2 * side) % ZN, (z + ZN - side) % ZN, (z + ZN - 3 * side) % ZN]
    guest_z = [z, (z + ZN - 2 * side) % ZN, host_z[2], host_z[3]]
    middle = (z == 1) | (z == 2)
    edge = (z == 0) | (z == 3)
    other = 1 - head

    def device(to_x, to_z, to_y):
        return (to_x * 32 + to_z * 4 + to_y, head)

    def remote(src, dst, send, recv, to):
        return pltpu.make_async_remote_copy(
            src_ref=src, dst_ref=dst, send_sem=send, recv_sem=recv, device_id=to, device_id_type=MESH
        )

    mine = [
        pltpu.make_async_copy(v_hbm, vraw, local_sem.at[0]),
        pltpu.make_async_copy(k_hbm, kv.at[0, y, pl.ds(0, BLK)], local_sem.at[1]),
        pltpu.make_async_copy(q_hbm, qbuf.at[0], local_sem.at[2]),
        pltpu.make_async_copy(
            w_hbm.at[:, pl.ds(pl.multiple_of(head * COLS, COLS), COLS)], wbuf.at[0], local_sem.at[3]
        ),
        pltpu.make_async_copy(picks_hbm, picks, local_sem.at[4]),
    ]
    row_peers = [(d, device(x, z, (y + d) % YN)) for d in (2, 1, 3)]
    pair_peer = device(x, pair_z, y)
    x_peers = [device((x + d) % XN, z, y) for d in range(1, XN)]
    greeted = [to for _, to in row_peers] + [pair_peer]
    greeted += [device(x, to_z, y) for to_z in host_z[1:] + guest_z[1:2]] + x_peers + [(ctx, other)]
    barrier = pltpu.get_barrier_semaphore()
    for to in greeted:
        pl.semaphore_signal(barrier, inc=1, device_id=to, device_id_type=MESH)
    for copy in mine:
        copy.start()

    def visits(dx, k):
        return x >= dx if dx else host_z[k] // 2 < z // 2

    def hosts(dx, k):
        return x + dx < XN if dx else z // 2 < guest_z[k] // 2

    for dx in range(XN):
        for k in range(MATES):
            if dx or k:
                @pl.when(jnp.logical_not(hosts(dx, k) if dx else (x >= 1) | hosts(0, k)))
                def _():
                    qbuf[k * XN + dx] = jnp.zeros((BLK, BLK), jnp.bfloat16)

    mine[0].wait()
    kv[0, y, BLK:] = vraw[...].T
    mine[1].wait()
    mine[2].wait()
    pl.semaphore_wait(barrier, len(greeted))

    def row_copy(d, to):
        return remote(kv.at[0, y], kv.at[0, y], kv_send.at[0, d], kv_recv.at[0, d], to)

    def pair_copy(part):
        rows = pl.ds(part * BLK, BLK)
        return remote(
            kv.at[0, y, rows], kv.at[1, y, rows], kv_send.at[part, 0], kv_recv.at[part, 0], pair_peer
        )

    def onward_copy(part, d, to):
        rows = pl.ds(part * BLK, BLK)
        at = kv.at[1, y, rows]
        return remote(at, at, kv_send.at[1 + part, d], kv_recv.at[1 + part, d], to)

    onward = [(part, d, to) for part in range(2) for d, to in row_peers]

    def z_copy(k):
        slot = k * XN
        return remote(qbuf.at[0], qbuf.at[slot], q_send.at[slot], q_recv.at[slot], device(x, host_z[k], y))

    def q_copy(dx, k):
        slot = k * XN + dx
        to = device((x + XN - dx) % XN, z, y)
        return remote(qbuf.at[k * XN], qbuf.at[slot], q_send.at[slot], q_recv.at[slot], to)

    def p_copies(slot, to):
        return [
            remote(pout.at[slot], pin.at[slot], p_send.at[slot, 0], p_recv.at[slot, 0], to),
            remote(sout.at[slot], sin.at[slot], p_send.at[slot, 1], p_recv.at[slot, 1], to),
        ]

    w_copy = remote(
        w_hbm.at[:, pl.ds(pl.multiple_of(other * COLS, COLS), COLS)],
        wbuf.at[1], h_send.at[0], h_recv.at[0], (ctx, other),
    )
    att_copy = remote(att.at[0], att.at[1], h_send.at[1], h_recv.at[1], (ctx, other))

    for part in range(2):
        pair_copy(part).start()
    for d, to in row_peers:
        row_copy(d, to).start()
    for k in NEAR:
        @pl.when((x >= 1) | visits(0, k))
        def _():
            z_copy(k).start()
    for dx in FORWARD:
        @pl.when(x >= dx)
        def _():
            q_copy(dx, 0).start()
    w_copy.start()

    def forward(k):
        @pl.when((x >= 1) | hosts(0, k))
        def _():
            z_copy(k).wait_recv()
        for dx in FORWARD:
            @pl.when(x >= dx)
            def _():
                q_copy(dx, k).start()

    for part in range(2):
        pair_copy(part).wait_recv()
        for d, to in row_peers:
            onward_copy(part, d, to).start()
    forward(NEAR[0])
    for k in NEAR[1:]:
        forward(k)

    def attend(k):
        queries = qbuf[k * XN:(k + 1) * XN].reshape(XN * BLK, BLK)
        keys = jnp.concatenate([kv[i, :, 0:BLK].reshape(CHUNK, BLK) for i in range(2)], axis=0)
        scores = lax.dot_general(
            keys, queries, (((1,), (1,)), ((), ())), preferred_element_type=jnp.float32
        )
        if k == 0:
            key = lax.broadcasted_iota(jnp.int32, (2 * CHUNK, BLK), 0)
            token = lax.broadcasted_iota(jnp.int32, (2 * CHUNK, BLK), 1)
            last = jnp.where(key < CHUNK, y * BLK + token, jnp.where(pair_z < z, 2 * CHUNK, -1))
            own = jnp.where(key <= last, scores[:, 0:BLK], NEGATIVE)
            scores = jnp.concatenate([own, scores[:, BLK:]], axis=1)
        high = jnp.max(scores, axis=0, keepdims=True)
        weights = jnp.exp2((scores - high) * RATE)
        part = jnp.sum(weights, axis=0, keepdims=True)
        values = jnp.concatenate([kv[i, b, BLK:] for i in range(2) for b in range(YN)], axis=1)
        numer = jnp.dot(values, weights.astype(jnp.bfloat16), preferred_element_type=jnp.float32)
        if k == 0:
            top[...] = high[:, 0:BLK]
            total[...] = part[:, 0:BLK]
            acc[...] = numer[:, 0:BLK]
        for dx in range(XN):
            if (dx, k) == (0, 0):
                continue
            slot = k * XN + dx
            lanes = slice(dx * BLK, (dx + 1) * BLK)
            pout[slot] = (numer[:, lanes] / part[:, lanes]).astype(jnp.bfloat16)
            sout[slot, 0:1] = high[:, lanes]
            sout[slot, 1:2] = part[:, lanes]

    def serve(k):
        for dx in range(1, XN):
            @pl.when(hosts(dx, k))
            def _():
                q_copy(dx, k).wait_recv()
        attend(k)
        for dx in (2, 3, 1, 0):
            if (dx, k) != (0, 0):
                @pl.when(hosts(dx, k))
                def _():
                    for copy in p_copies(k * XN + dx, device((x + dx) % XN, guest_z[k], y)):
                        copy.start()

    for d, to in row_peers:
        row_copy(d, to).wait_recv()
    for hop in onward:
        onward_copy(*hop).wait_recv()
    turns = [(0, edge), (3, jnp.logical_not(middle)), (1, x >= 0), (2, x >= 0), (0, jnp.logical_not(edge)), (3, middle)]
    for k, now in turns:
        @pl.when(now & ((x + 1 < XN) | hosts(0, k)) if k else now)
        def _():
            serve(k)

    mine[4].wait()
    first_pick, second_pick = picks[0, 0, ctx], picks[0, 1, ctx]

    def combine(k, dxs):
        slots = [k * XN + dx for dx in dxs]
        theirs = []
        for dx, slot in zip(dxs, slots):
            for copy in p_copies(slot, (ctx, head)):
                copy.wait_recv()
            score = sin[slot, 0:1]
            which = 2 * (x - dx) + host_z[k] // 4
            wanted = (first_pick == which) | (second_pick == which) | (which == span)
            theirs.append(jnp.where(wanted, score, NEGATIVE))
        ours = top[...]
        high = ours
        for score in theirs:
            high = jnp.maximum(high, score)
        fade = jnp.exp2((ours - high) * RATE)
        part = total[...] * fade
        numer = acc[...] * fade
        for score, slot in zip(theirs, slots):
            share = sin[slot, 1:2] * jnp.exp2((score - high) * RATE)
            part = part + share
            numer = numer + pin[slot].astype(jnp.float32) * share
        top[...] = high
        total[...] = part
        acc[...] = numer

    for k in SERVE:
        if k:
            @pl.when(visits(0, k))
            def _():
                combine(k, [0])

        for far_x in range(1, XN):
            @pl.when(x == far_x)
            def _():
                combine(k, range(1, far_x + 1))

    att[0] = (acc[...] / total[...]).T.astype(jnp.bfloat16)
    att_copy.start()
    mine[3].wait()
    w_copy.wait_recv()
    wide = 512
    columns = [slice(n, n + wide) for n in range(0, COLS, wide)]
    for part in columns:
        term[:, part] = jnp.dot(att[0], wbuf[0, :, part], preferred_element_type=jnp.float32)
    att_copy.wait_recv()
    for part in columns:
        more = jnp.dot(att[1], wbuf[1, :, part], preferred_element_type=jnp.float32)
        out_ref[:, part] = (term[:, part] + more).astype(jnp.bfloat16)

    for part in range(2):
        pair_copy(part).wait_send()
    for d, to in row_peers:
        row_copy(d, to).wait_send()
    for hop in onward:
        onward_copy(*hop).wait_send()
    for k in range(MATES):
        for dx in range(XN):
            if dx:
                @pl.when(x >= dx)
                def _():
                    q_copy(dx, k).wait_send()
            elif k:
                @pl.when((x >= 1) | visits(0, k))
                def _():
                    z_copy(k).wait_send()
            if dx or k:
                @pl.when(hosts(dx, k))
                def _():
                    for copy in p_copies(k * XN + dx, device((x + dx) % XN, guest_z[k], y)):
                        copy.wait_send()
    w_copy.wait_send()
    att_copy.wait_send()


def local(queries, keys, values, picks, out_weight):
    hbm = pl.BlockSpec(memory_space=pltpu.HBM)
    dma = pltpu.SemaphoreType.DMA
    bf16, f32 = jnp.bfloat16, jnp.float32
    return pl.pallas_call(
        kernel,
        out_shape=pltpu.VMEM((BLK, COLS), bf16),
        in_specs=[hbm] * 5,
        out_specs=pl.BlockSpec(memory_space=pltpu.VMEM),
        scratch_shapes=[
            pltpu.SMEM((1, 2, BLK), jnp.int32),
            pltpu.VMEM((2, YN, 2 * BLK, BLK), bf16),
            pltpu.VMEM((SLOTS, BLK, BLK), bf16),
            pltpu.VMEM((BLK, BLK), bf16),
            pltpu.VMEM((SLOTS, BLK, BLK), bf16),
            pltpu.VMEM((SLOTS, 2, BLK), f32),
            pltpu.VMEM((SLOTS, BLK, BLK), bf16),
            pltpu.VMEM((SLOTS, 2, BLK), f32),
            pltpu.VMEM((2, BLK, COLS), bf16),
            pltpu.VMEM((2, BLK, BLK), bf16),
            pltpu.VMEM((BLK, COLS), f32),
            pltpu.VMEM((1, BLK), f32),
            pltpu.VMEM((1, BLK), f32),
            pltpu.VMEM((BLK, BLK), f32),
            dma((5,)),
            dma((3, YN)),
            dma((3, YN)),
            dma((SLOTS,)),
            dma((SLOTS,)),
            dma((SLOTS, 2)),
            dma((SLOTS, 2)),
            dma((2,)),
            dma((2,)),
        ],
        compiler_params=pltpu.CompilerParams(
            collective_id=0, has_side_effects=True, vmem_limit_bytes=56 * 1024 * 1024
        ),
        cost_estimate=pl.CostEstimate(flops=2**30, bytes_accessed=2**22, transcendentals=2**21),
    )(queries, keys, values, jnp.swapaxes(picks, 1, 2), out_weight)


def solution(mesh):
    placed = (
        P("ctx", "head"),
        P("ctx", "head"),
        P("ctx", "head"),
        P("head", None, None),
        P("head", None),
    )
    return jax.shard_map(
        local, mesh=mesh, in_specs=placed, out_specs=P("ctx", "head"), check_vma=False
    )
```

```python
import math

import jax
import jax.numpy as jnp
from jax import lax
from jax.experimental import pallas as pl
from jax.experimental.pallas import tpu as pltpu
from jax.sharding import PartitionSpec as P

BLK = 128
XN = 4
YN = 4
ZN = 8
MATES = 4
NEAR = (3, 1, 2)
FORWARD = (3, 2, 1)
SERVE = (3, 1, 2, 0)
SLOTS = MATES * XN
CHUNK = YN * BLK
COLS = 2048
NEGATIVE = -1e30
RATE = math.log2(math.e) / math.sqrt(128.0)
MESH = pl.DeviceIdType.MESH


def kernel(
    q_hbm, k_hbm, v_hbm, picks_hbm, w_hbm, out_ref,
    picks, kv, qbuf, vraw, pout, sout, pin, sin, wbuf, att, term, top, total, acc,
    local_sem, kv_send, kv_recv, q_send, q_recv, p_send, p_recv, h_send, h_recv,
):
    ctx = lax.axis_index("ctx")
    head = lax.axis_index("head")
    x = ctx // 32
    z = (ctx % 32) // 4
    y = ctx % 4
    span = 2 * x + z // 4
    side = 1 - 2 * (z % 2)
    pair_z = z + side
    host_z = [z, (z + ZN + 2 * side) % ZN, (z + ZN - side) % ZN, (z + ZN - 3 * side) % ZN]
    guest_z = [z, (z + ZN - 2 * side) % ZN, host_z[2], host_z[3]]
    middle = (z == 1) | (z == 2)
    edge = (z == 0) | (z == 3)
    other = 1 - head

    def device(to_x, to_z, to_y):
        return (to_x * 32 + to_z * 4 + to_y, head)

    def remote(src, dst, send, recv, to):
        return pltpu.make_async_remote_copy(
            src_ref=src, dst_ref=dst, send_sem=send, recv_sem=recv, device_id=to, device_id_type=MESH
        )

    mine = [
        pltpu.make_async_copy(v_hbm, vraw, local_sem.at[0]),
        pltpu.make_async_copy(k_hbm, kv.at[0, y, pl.ds(0, BLK)], local_sem.at[1]),
        pltpu.make_async_copy(q_hbm, qbuf.at[0], local_sem.at[2]),
        pltpu.make_async_copy(
            w_hbm.at[:, pl.ds(pl.multiple_of(head * COLS, COLS), COLS)], wbuf.at[0], local_sem.at[3]
        ),
        pltpu.make_async_copy(picks_hbm, picks, local_sem.at[4]),
    ]
    row_peers = [(d, device(x, z, (y + d) % YN)) for d in (2, 1, 3)]
    pair_peer = device(x, pair_z, y)
    x_peers = [device((x + d) % XN, z, y) for d in range(1, XN)]
    greeted = [to for _, to in row_peers] + [pair_peer]
    greeted += [device(x, to_z, y) for to_z in host_z[1:] + guest_z[1:2]] + x_peers + [(ctx, other)]
    barrier = pltpu.get_barrier_semaphore()
    for to in greeted:
        pl.semaphore_signal(barrier, inc=1, device_id=to, device_id_type=MESH)
    for copy in mine:
        copy.start()

    def visits(dx, k):
        return x >= dx if dx else host_z[k] // 2 < z // 2

    def hosts(dx, k):
        return x + dx < XN if dx else z // 2 < guest_z[k] // 2

    for dx in range(XN):
        for k in range(MATES):
            if dx or k:
                @pl.when(jnp.logical_not(hosts(dx, k) if dx else (x >= 1) | hosts(0, k)))
                def _():
                    qbuf[k * XN + dx] = jnp.zeros((BLK, BLK), jnp.bfloat16)

    mine[0].wait()
    kv[0, y, BLK:] = vraw[...].T
    mine[1].wait()
    mine[2].wait()
    pl.semaphore_wait(barrier, len(greeted))

    def row_copy(d, to):
        return remote(kv.at[0, y], kv.at[0, y], kv_send.at[0, d], kv_recv.at[0, d], to)

    def pair_copy(part):
        rows = pl.ds(part * BLK, BLK)
        return remote(
            kv.at[0, y, rows], kv.at[1, y, rows], kv_send.at[part, 0], kv_recv.at[part, 0], pair_peer
        )

    def onward_copy(part, d, to):
        rows = pl.ds(part * BLK, BLK)
        at = kv.at[1, y, rows]
        return remote(at, at, kv_send.at[1 + part, d], kv_recv.at[1 + part, d], to)

    onward = [(part, d, to) for part in range(2) for d, to in row_peers]

    def z_copy(k):
        slot = k * XN
        return remote(qbuf.at[0], qbuf.at[slot], q_send.at[slot], q_recv.at[slot], device(x, host_z[k], y))

    def q_copy(dx, k):
        slot = k * XN + dx
        to = device((x + XN - dx) % XN, z, y)
        return remote(qbuf.at[k * XN], qbuf.at[slot], q_send.at[slot], q_recv.at[slot], to)

    def p_copies(slot, to):
        return [
            remote(pout.at[slot], pin.at[slot], p_send.at[slot, 0], p_recv.at[slot, 0], to),
            remote(sout.at[slot], sin.at[slot], p_send.at[slot, 1], p_recv.at[slot, 1], to),
        ]

    w_copy = remote(
        w_hbm.at[:, pl.ds(pl.multiple_of(other * COLS, COLS), COLS)],
        wbuf.at[1], h_send.at[0], h_recv.at[0], (ctx, other),
    )
    att_copy = remote(att.at[0], att.at[1], h_send.at[1], h_recv.at[1], (ctx, other))

    for part in range(2):
        pair_copy(part).start()
    for d, to in row_peers:
        row_copy(d, to).start()
    for k in NEAR:
        @pl.when((x >= 1) | visits(0, k))
        def _():
            z_copy(k).start()
    for dx in FORWARD:
        @pl.when(x >= dx)
        def _():
            q_copy(dx, 0).start()
    w_copy.start()

    def forward(k):
        @pl.when((x >= 1) | hosts(0, k))
        def _():
            z_copy(k).wait_recv()
        for dx in FORWARD:
            @pl.when(x >= dx)
            def _():
                q_copy(dx, k).start()

    for part in range(2):
        pair_copy(part).wait_recv()
        for d, to in row_peers:
            onward_copy(part, d, to).start()
    forward(NEAR[0])
    for k in NEAR[1:]:
        forward(k)

    def attend(k):
        queries = qbuf[k * XN:(k + 1) * XN].reshape(XN * BLK, BLK)
        keys = jnp.concatenate([kv[i, :, 0:BLK].reshape(CHUNK, BLK) for i in range(2)], axis=0)
        scores = lax.dot_general(
            keys, queries, (((1,), (1,)), ((), ())), preferred_element_type=jnp.float32
        )
        if k == 0:
            key = lax.broadcasted_iota(jnp.int32, (2 * CHUNK, BLK), 0)
            token = lax.broadcasted_iota(jnp.int32, (2 * CHUNK, BLK), 1)
            last = jnp.where(key < CHUNK, y * BLK + token, jnp.where(pair_z < z, 2 * CHUNK, -1))
            own = jnp.where(key <= last, scores[:, 0:BLK], NEGATIVE)
            scores = jnp.concatenate([own, scores[:, BLK:]], axis=1)
        high = jnp.max(scores, axis=0, keepdims=True)
        weights = jnp.exp2((scores - high) * RATE)
        part = jnp.sum(weights, axis=0, keepdims=True)
        values = jnp.concatenate([kv[i, b, BLK:] for i in range(2) for b in range(YN)], axis=1)
        numer = jnp.dot(values, weights.astype(jnp.bfloat16), preferred_element_type=jnp.float32)
        if k == 0:
            top[...] = high[:, 0:BLK]
            total[...] = part[:, 0:BLK]
            acc[...] = numer[:, 0:BLK]
        for dx in (2, 3, 1, 0):
            if (dx, k) == (0, 0):
                continue
            slot = k * XN + dx
            lanes = slice(dx * BLK, (dx + 1) * BLK)
            pout[slot] = (numer[:, lanes] / part[:, lanes]).astype(jnp.bfloat16)
            sout[slot, 0:1] = high[:, lanes]
            sout[slot, 1:2] = part[:, lanes]

            @pl.when(hosts(dx, k))
            def _():
                for copy in p_copies(slot, device((x + dx) % XN, guest_z[k], y)):
                    copy.start()

    def serve(k):
        for dx in range(1, XN):
            @pl.when(hosts(dx, k))
            def _():
                q_copy(dx, k).wait_recv()
        attend(k)

    for d, to in row_peers:
        row_copy(d, to).wait_recv()
    for hop in onward:
        onward_copy(*hop).wait_recv()
    turns = [(0, edge), (3, jnp.logical_not(middle)), (1, x >= 0), (2, x >= 0), (0, jnp.logical_not(edge)), (3, middle)]
    for k, now in turns:
        @pl.when(now & ((x + 1 < XN) | hosts(0, k)) if k else now)
        def _():
            serve(k)

    mine[4].wait()
    first_pick, second_pick = picks[0, 0, ctx], picks[0, 1, ctx]

    def combine(k, dxs):
        slots = [k * XN + dx for dx in dxs]
        theirs = []
        for dx, slot in zip(dxs, slots):
            for copy in p_copies(slot, (ctx, head)):
                copy.wait_recv()
            score = sin[slot, 0:1]
            which = 2 * (x - dx) + host_z[k] // 4
            wanted = (first_pick == which) | (second_pick == which) | (which == span)
            theirs.append(jnp.where(wanted, score, NEGATIVE))
        ours = top[...]
        high = ours
        for score in theirs:
            high = jnp.maximum(high, score)
        fade = jnp.exp2((ours - high) * RATE)
        part = total[...] * fade
        numer = acc[...] * fade
        for score, slot in zip(theirs, slots):
            share = sin[slot, 1:2] * jnp.exp2((score - high) * RATE)
            part = part + share
            numer = numer + pin[slot].astype(jnp.float32) * share
        top[...] = high
        total[...] = part
        acc[...] = numer

    for k in SERVE:
        if k:
            @pl.when(visits(0, k))
            def _():
                combine(k, [0])

        for far_x in range(1, XN):
            @pl.when(x == far_x)
            def _():
                combine(k, range(1, far_x + 1))

    att[0] = (acc[...] / total[...]).T.astype(jnp.bfloat16)
    att_copy.start()
    mine[3].wait()
    w_copy.wait_recv()
    wide = 512
    columns = [slice(n, n + wide) for n in range(0, COLS, wide)]
    for part in columns:
        term[:, part] = jnp.dot(att[0], wbuf[0, :, part], preferred_element_type=jnp.float32)
    att_copy.wait_recv()
    for part in columns:
        more = jnp.dot(att[1], wbuf[1, :, part], preferred_element_type=jnp.float32)
        out_ref[:, part] = (term[:, part] + more).astype(jnp.bfloat16)

    for part in range(2):
        pair_copy(part).wait_send()
    for d, to in row_peers:
        row_copy(d, to).wait_send()
    for hop in onward:
        onward_copy(*hop).wait_send()
    for k in range(MATES):
        for dx in range(XN):
            if dx:
                @pl.when(x >= dx)
                def _():
                    q_copy(dx, k).wait_send()
            elif k:
                @pl.when((x >= 1) | visits(0, k))
                def _():
                    z_copy(k).wait_send()
            if dx or k:
                @pl.when(hosts(dx, k))
                def _():
                    for copy in p_copies(k * XN + dx, device((x + dx) % XN, guest_z[k], y)):
                        copy.wait_send()
    w_copy.wait_send()
    att_copy.wait_send()


def local(queries, keys, values, picks, out_weight):
    hbm = pl.BlockSpec(memory_space=pltpu.HBM)
    dma = pltpu.SemaphoreType.DMA
    bf16, f32 = jnp.bfloat16, jnp.float32
    return pl.pallas_call(
        kernel,
        out_shape=pltpu.VMEM((BLK, COLS), bf16),
        in_specs=[hbm] * 5,
        out_specs=pl.BlockSpec(memory_space=pltpu.VMEM),
        scratch_shapes=[
            pltpu.SMEM((1, 2, BLK), jnp.int32),
            pltpu.VMEM((2, YN, 2 * BLK, BLK), bf16),
            pltpu.VMEM((SLOTS, BLK, BLK), bf16),
            pltpu.VMEM((BLK, BLK), bf16),
            pltpu.VMEM((SLOTS, BLK, BLK), bf16),
            pltpu.VMEM((SLOTS, 2, BLK), f32),
            pltpu.VMEM((SLOTS, BLK, BLK), bf16),
            pltpu.VMEM((SLOTS, 2, BLK), f32),
            pltpu.VMEM((2, BLK, COLS), bf16),
            pltpu.VMEM((2, BLK, BLK), bf16),
            pltpu.VMEM((BLK, COLS), f32),
            pltpu.VMEM((1, BLK), f32),
            pltpu.VMEM((1, BLK), f32),
            pltpu.VMEM((BLK, BLK), f32),
            dma((5,)),
            dma((3, YN)),
            dma((3, YN)),
            dma((SLOTS,)),
            dma((SLOTS,)),
            dma((SLOTS, 2)),
            dma((SLOTS, 2)),
            dma((2,)),
            dma((2,)),
        ],
        compiler_params=pltpu.CompilerParams(
            collective_id=0, has_side_effects=True, vmem_limit_bytes=56 * 1024 * 1024
        ),
        cost_estimate=pl.CostEstimate(flops=2**30, bytes_accessed=2**22, transcendentals=2**21),
    )(queries, keys, values, jnp.swapaxes(picks, 1, 2), out_weight)


def solution(mesh):
    placed = (
        P("ctx", "head"),
        P("ctx", "head"),
        P("ctx", "head"),
        P("head", None, None),
        P("head", None),
    )
    return jax.shard_map(
        local, mesh=mesh, in_specs=placed, out_specs=P("ctx", "head"), check_vma=False
    )
```

```python
import math

import jax
import jax.numpy as jnp
from jax import lax
from jax.experimental import pallas as pl
from jax.experimental.pallas import tpu as pltpu
from jax.sharding import PartitionSpec as P

BLK = 128
XN = 4
YN = 4
ZN = 8
MATES = 4
NEAR = (3, 1, 2)
FORWARD = (3, 2, 1)
SERVE = (3, 1, 2, 0)
SLOTS = MATES * XN
CHUNK = YN * BLK
COLS = 2048
NEGATIVE = -1e30
RATE = math.log2(math.e) / math.sqrt(128.0)
MESH = pl.DeviceIdType.MESH


def kernel(
    q_hbm, k_hbm, v_hbm, picks_hbm, w_hbm, out_ref,
    picks, kv, qbuf, vraw, pout, sout, pin, sin, wbuf, att, term, top, total, acc,
    local_sem, kv_send, kv_recv, q_send, q_recv, p_send, p_recv, h_send, h_recv,
):
    ctx = lax.axis_index("ctx")
    head = lax.axis_index("head")
    x = ctx // 32
    z = (ctx % 32) // 4
    y = ctx % 4
    span = 2 * x + z // 4
    side = 1 - 2 * (z % 2)
    pair_z = z + side
    host_z = [z, (z + ZN + 2 * side) % ZN, (z + ZN - side) % ZN, (z + ZN - 3 * side) % ZN]
    guest_z = [z, (z + ZN - 2 * side) % ZN, host_z[2], host_z[3]]
    middle = (z == 1) | (z == 2)
    edge = (z == 0) | (z == 3)
    other = 1 - head

    def device(to_x, to_z, to_y):
        return (to_x * 32 + to_z * 4 + to_y, head)

    def remote(src, dst, send, recv, to):
        return pltpu.make_async_remote_copy(
            src_ref=src, dst_ref=dst, send_sem=send, recv_sem=recv, device_id=to, device_id_type=MESH
        )

    mine = [
        pltpu.make_async_copy(v_hbm, vraw, local_sem.at[0]),
        pltpu.make_async_copy(k_hbm, kv.at[0, y, pl.ds(0, BLK)], local_sem.at[1]),
        pltpu.make_async_copy(q_hbm, qbuf.at[0], local_sem.at[2]),
        pltpu.make_async_copy(
            w_hbm.at[:, pl.ds(pl.multiple_of(head * COLS, COLS), COLS)], wbuf.at[0], local_sem.at[3]
        ),
        pltpu.make_async_copy(picks_hbm, picks, local_sem.at[4]),
    ]
    row_peers = [(d, device(x, z, (y + d) % YN)) for d in (2, 1, 3)]
    pair_peer = device(x, pair_z, y)
    x_peers = [device((x + d) % XN, z, y) for d in range(1, XN)]
    greeted = [to for _, to in row_peers] + [pair_peer]
    greeted += [device(x, to_z, y) for to_z in host_z[1:] + guest_z[1:2]] + x_peers + [(ctx, other)]
    barrier = pltpu.get_barrier_semaphore()
    for to in greeted:
        pl.semaphore_signal(barrier, inc=1, device_id=to, device_id_type=MESH)
    for copy in mine:
        copy.start()

    def visits(dx, k):
        return x >= dx if dx else host_z[k] // 2 < z // 2

    def hosts(dx, k):
        return x + dx < XN if dx else z // 2 < guest_z[k] // 2

    for dx in range(XN):
        for k in range(MATES):
            if dx or k:
                @pl.when(jnp.logical_not(hosts(dx, k) if dx else (x >= 1) | hosts(0, k)))
                def _():
                    qbuf[k * XN + dx] = jnp.zeros((BLK, BLK), jnp.bfloat16)

    mine[0].wait()
    kv[0, y, BLK:] = vraw[...].T
    mine[1].wait()
    mine[2].wait()
    pl.semaphore_wait(barrier, len(greeted))

    def row_copy(d, to):
        return remote(kv.at[0, y], kv.at[0, y], kv_send.at[0, d], kv_recv.at[0, d], to)

    def pair_copy(part):
        rows = pl.ds(part * BLK, BLK)
        return remote(
            kv.at[0, y, rows], kv.at[1, y, rows], kv_send.at[part, 0], kv_recv.at[part, 0], pair_peer
        )

    def onward_copy(part, d, to):
        rows = pl.ds(part * BLK, BLK)
        at = kv.at[1, y, rows]
        return remote(at, at, kv_send.at[1 + part, d], kv_recv.at[1 + part, d], to)

    onward = [(part, d, to) for part in range(2) for d, to in row_peers]

    def z_copy(k):
        slot = k * XN
        return remote(qbuf.at[0], qbuf.at[slot], q_send.at[slot], q_recv.at[slot], device(x, host_z[k], y))

    def q_copy(dx, k):
        slot = k * XN + dx
        to = device((x + XN - dx) % XN, z, y)
        return remote(qbuf.at[k * XN], qbuf.at[slot], q_send.at[slot], q_recv.at[slot], to)

    def p_copies(slot, to):
        return [
            remote(pout.at[slot], pin.at[slot], p_send.at[slot, 0], p_recv.at[slot, 0], to),
            remote(sout.at[slot], sin.at[slot], p_send.at[slot, 1], p_recv.at[slot, 1], to),
        ]

    w_copy = remote(
        w_hbm.at[:, pl.ds(pl.multiple_of(other * COLS, COLS), COLS)],
        wbuf.at[1], h_send.at[0], h_recv.at[0], (ctx, other),
    )
    att_copy = remote(att.at[0], att.at[1], h_send.at[1], h_recv.at[1], (ctx, other))

    for part in range(2):
        pair_copy(part).start()
    for d, to in row_peers:
        row_copy(d, to).start()
    for k in NEAR:
        @pl.when((x >= 1) | visits(0, k))
        def _():
            z_copy(k).start()
    for dx in FORWARD:
        @pl.when(x >= dx)
        def _():
            q_copy(dx, 0).start()
    w_copy.start()

    def forward(k):
        @pl.when((x >= 1) | hosts(0, k))
        def _():
            z_copy(k).wait_recv()
        for dx in FORWARD:
            @pl.when(x >= dx)
            def _():
                q_copy(dx, k).start()

    for part in range(2):
        pair_copy(part).wait_recv()
        for d, to in row_peers:
            onward_copy(part, d, to).start()
    forward(NEAR[0])
    for k in NEAR[1:]:
        forward(k)

    def attend(k):
        queries = qbuf[k * XN:(k + 1) * XN].reshape(XN * BLK, BLK)
        keys = jnp.concatenate([kv[i, :, 0:BLK].reshape(CHUNK, BLK) for i in range(2)], axis=0)
        scores = lax.dot_general(
            keys, queries, (((1,), (1,)), ((), ())), preferred_element_type=jnp.float32
        )
        if k == 0:
            key = lax.broadcasted_iota(jnp.int32, (2 * CHUNK, BLK), 0)
            token = lax.broadcasted_iota(jnp.int32, (2 * CHUNK, BLK), 1)
            last = jnp.where(key < CHUNK, y * BLK + token, jnp.where(pair_z < z, 2 * CHUNK, -1))
            own = jnp.where(key <= last, scores[:, 0:BLK], NEGATIVE)
            scores = jnp.concatenate([own, scores[:, BLK:]], axis=1)
        high = jnp.max(scores, axis=0, keepdims=True)
        weights = jnp.exp2((scores - high) * RATE)
        part = jnp.sum(weights, axis=0, keepdims=True)
        values = jnp.concatenate([kv[i, b, BLK:] for i in range(2) for b in range(YN)], axis=1)
        numer = jnp.dot(values, weights.astype(jnp.bfloat16), preferred_element_type=jnp.float32)
        if k == 0:
            top[...] = high[:, 0:BLK] * RATE
            total[...] = part[:, 0:BLK]
            acc[...] = numer[:, 0:BLK]
        for dx in range(XN):
            if (dx, k) == (0, 0):
                continue
            slot = k * XN + dx
            lanes = slice(dx * BLK, (dx + 1) * BLK)
            pout[slot] = (numer[:, lanes] / part[:, lanes]).astype(jnp.bfloat16)
            sout[slot] = high[:, lanes] * RATE + jnp.log2(part[:, lanes])

    def serve(k):
        for dx in range(1, XN):
            @pl.when(hosts(dx, k))
            def _():
                q_copy(dx, k).wait_recv()
        attend(k)
        for dx in (2, 3, 1, 0):
            if (dx, k) != (0, 0):
                @pl.when(hosts(dx, k))
                def _():
                    for copy in p_copies(k * XN + dx, device((x + dx) % XN, guest_z[k], y)):
                        copy.start()

    for d, to in row_peers:
        row_copy(d, to).wait_recv()
    for hop in onward:
        onward_copy(*hop).wait_recv()
    turns = [(0, edge), (3, jnp.logical_not(middle)), (1, x >= 0), (2, x >= 0), (0, jnp.logical_not(edge)), (3, middle)]
    for k, now in turns:
        @pl.when(now & ((x + 1 < XN) | hosts(0, k)) if k else now)
        def _():
            serve(k)

    mine[4].wait()
    first_pick, second_pick = picks[0, 0, ctx], picks[0, 1, ctx]

    def combine(k, dxs):
        slots = [k * XN + dx for dx in dxs]
        theirs = []
        for dx, slot in zip(dxs, slots):
            for copy in p_copies(slot, (ctx, head)):
                copy.wait_recv()
            score = sin[slot, 0:1]
            which = 2 * (x - dx) + host_z[k] // 4
            wanted = (first_pick == which) | (second_pick == which) | (which == span)
            theirs.append(jnp.where(wanted, score, NEGATIVE))
        ours = top[...]
        high = ours
        for score in theirs:
            high = jnp.maximum(high, score)
        fade = jnp.exp2(ours - high)
        part = total[...] * fade
        numer = acc[...] * fade
        for score, slot in zip(theirs, slots):
            share = jnp.exp2(score - high)
            part = part + share
            numer = numer + pin[slot].astype(jnp.float32) * share
        top[...] = high
        total[...] = part
        acc[...] = numer

    for k in SERVE:
        if k:
            @pl.when(visits(0, k))
            def _():
                combine(k, [0])

        for far_x in range(1, XN):
            @pl.when(x == far_x)
            def _():
                combine(k, range(1, far_x + 1))

    att[0] = (acc[...] / total[...]).T.astype(jnp.bfloat16)
    att_copy.start()
    mine[3].wait()
    w_copy.wait_recv()
    wide = 512
    columns = [slice(n, n + wide) for n in range(0, COLS, wide)]
    for part in columns:
        term[:, part] = jnp.dot(att[0], wbuf[0, :, part], preferred_element_type=jnp.float32)
    att_copy.wait_recv()
    for part in columns:
        more = jnp.dot(att[1], wbuf[1, :, part], preferred_element_type=jnp.float32)
        out_ref[:, part] = (term[:, part] + more).astype(jnp.bfloat16)

    for part in range(2):
        pair_copy(part).wait_send()
    for d, to in row_peers:
        row_copy(d, to).wait_send()
    for hop in onward:
        onward_copy(*hop).wait_send()
    for k in range(MATES):
        for dx in range(XN):
            if dx:
                @pl.when(x >= dx)
                def _():
                    q_copy(dx, k).wait_send()
            elif k:
                @pl.when((x >= 1) | visits(0, k))
                def _():
                    z_copy(k).wait_send()
            if dx or k:
                @pl.when(hosts(dx, k))
                def _():
                    for copy in p_copies(k * XN + dx, device((x + dx) % XN, guest_z[k], y)):
                        copy.wait_send()
    w_copy.wait_send()
    att_copy.wait_send()


def local(queries, keys, values, picks, out_weight):
    hbm = pl.BlockSpec(memory_space=pltpu.HBM)
    dma = pltpu.SemaphoreType.DMA
    bf16, f32 = jnp.bfloat16, jnp.float32
    return pl.pallas_call(
        kernel,
        out_shape=pltpu.VMEM((BLK, COLS), bf16),
        in_specs=[hbm] * 5,
        out_specs=pl.BlockSpec(memory_space=pltpu.VMEM),
        scratch_shapes=[
            pltpu.SMEM((1, 2, BLK), jnp.int32),
            pltpu.VMEM((2, YN, 2 * BLK, BLK), bf16),
            pltpu.VMEM((SLOTS, BLK, BLK), bf16),
            pltpu.VMEM((BLK, BLK), bf16),
            pltpu.VMEM((SLOTS, BLK, BLK), bf16),
            pltpu.VMEM((SLOTS, 1, BLK), f32),
            pltpu.VMEM((SLOTS, BLK, BLK), bf16),
            pltpu.VMEM((SLOTS, 1, BLK), f32),
            pltpu.VMEM((2, BLK, COLS), bf16),
            pltpu.VMEM((2, BLK, BLK), bf16),
            pltpu.VMEM((BLK, COLS), f32),
            pltpu.VMEM((1, BLK), f32),
            pltpu.VMEM((1, BLK), f32),
            pltpu.VMEM((BLK, BLK), f32),
            dma((5,)),
            dma((3, YN)),
            dma((3, YN)),
            dma((SLOTS,)),
            dma((SLOTS,)),
            dma((SLOTS, 2)),
            dma((SLOTS, 2)),
            dma((2,)),
            dma((2,)),
        ],
        compiler_params=pltpu.CompilerParams(
            collective_id=0, has_side_effects=True, vmem_limit_bytes=56 * 1024 * 1024
        ),
        cost_estimate=pl.CostEstimate(flops=2**30, bytes_accessed=2**22, transcendentals=2**21),
    )(queries, keys, values, jnp.swapaxes(picks, 1, 2), out_weight)


def solution(mesh):
    placed = (
        P("ctx", "head"),
        P("ctx", "head"),
        P("ctx", "head"),
        P("head", None, None),
        P("head", None),
    )
    return jax.shard_map(
        local, mesh=mesh, in_specs=placed, out_specs=P("ctx", "head"), check_vma=False
    )
```
